256 devices in a mesh: dp: 8 (over x, core), fsdp: 32 (over y, z).
Axes of the slice: x: 4, y: 4, z: 8, core: 2. Of those that a mesh axis runs over, the one named last changes fastest.
Arguments:
- gradients: bfloat16 [8, 512, 65536], P('dp', 'fsdp'), may hold values from -36 to 36
Outputs:
- update: bfloat16 [512, 32, 8, 256], P('fsdp', None, 'dp')
The draws below stay inside these ranges and needn't reach their ends.
All inputs are finite; a program needn't handle non-finite values.
Results may differ from the reference program's by a relative error of at most 0.0077.
Values may be sent and summed in bfloat16 or wider, within the bound.
No kernel may reach another device: no remote copies, remote signals or barrier semaphores. Data moves between devices by JAX's collectives and lax.ppermute only.
A program may use at most 64 MiB of HBM per device.

```python
import math
import jax
import jax.numpy as jnp
from jax import lax

BLOCK = 512
ITERS = 6
GROUPS = 8
BC = 4
D = 512
F = 65536
HALF = 256
N_FSDP = 32


def draw_gradients(key, part):
    key = jax.random.fold_in(key, 11)
    subkeys = jax.random.split(key, 4)
    row_scale = jnp.exp(jax.random.uniform(subkeys[0], (1, D, 1), minval=math.log(0.3), maxval=math.log(3.0)))
    col_scale = jnp.exp(jax.random.uniform(subkeys[1], (1, 1, F), minval=math.log(0.3), maxval=math.log(3.0)))
    noise = jnp.clip(jax.random.normal(subkeys[3], (GROUPS, D, F)), -4.0, 4.0)
    return (noise * row_scale * col_scale).astype(jnp.bfloat16)


def setup_inputs(seed: int = 0) -> dict:
    arg_keys = jax.random.split(jax.random.key(seed), 2)
    return {
        "gradients": draw_gradients(jax.random.fold_in(arg_keys[1], 71), 0),
    }


def inverse_root(statistic):
    identity = jnp.eye(statistic.shape[0], dtype=jnp.float32)
    trace_sum = jnp.trace(statistic)
    moment = statistic / trace_sum
    inverse = identity * trace_sum ** -0.25
    for iteration in range(ITERS):
        factor = (5.0 * identity - moment) * 0.25
        inverse = jnp.dot(inverse, factor, precision=lax.Precision.HIGHEST, preferred_element_type=jnp.float32)
        square = jnp.dot(factor, factor, precision=lax.Precision.HIGHEST, preferred_element_type=jnp.float32)
        fourth = jnp.dot(square, square, precision=lax.Precision.HIGHEST, preferred_element_type=jnp.float32)
        moment = jnp.dot(fourth, moment, precision=lax.Precision.HIGHEST, preferred_element_type=jnp.float32)
    return inverse


def reference(gradients):
    block_count = N_FSDP * BC

    def one_block(block_index):
        start = (block_index * BLOCK).astype(jnp.int32)
        block_grads = lax.dynamic_slice_in_dim(gradients, start, BLOCK, 2).astype(jnp.float32)
        left_stat = jnp.einsum('gik,gjk->ij', block_grads, block_grads) / (GROUPS * BLOCK)
        right_stat = jnp.einsum('gki,gkj->ij', block_grads, block_grads) / (GROUPS * BLOCK)
        left_root = inverse_root(left_stat).astype(jnp.bfloat16)
        right_root = inverse_root(right_stat).astype(jnp.bfloat16)
        mean_grad = (jnp.sum(block_grads, axis=0) / GROUPS).astype(jnp.bfloat16)
        right_part = jnp.dot(mean_grad, right_root, preferred_element_type=jnp.float32).astype(jnp.bfloat16)
        return jnp.dot(left_root, right_part, preferred_element_type=jnp.float32).astype(jnp.bfloat16)

    pieces = lax.map(one_block, jnp.arange(block_count, dtype=jnp.int32))
    pieces = pieces.reshape(N_FSDP, BC, D, 2, HALF)
    pieces = jnp.transpose(pieces, (2, 0, 1, 3, 4))
    return pieces.reshape(D, N_FSDP, GROUPS, HALF)
```

```python
import jax
import jax.numpy as jnp
from jax import lax
from jax.experimental import pallas as pl
from jax.experimental.pallas import tpu as pltpu
from jax.sharding import Mesh
from jax.sharding import PartitionSpec as P

ITERS = 6
GROUPS = 8
BLOCK = 512
PER_STRIP = 4
STRIPS = 32
HALF = 256
LANE = 128
STRIPS_PER_STEP = 8


def dot_nn(a, b):
    return lax.dot_general(a, b, (((1,), (0,)), ((), ())), preferred_element_type=jnp.float32)


def dot_nt(a, b):
    return lax.dot_general(a, b, (((1,), (1,)), ((), ())), preferred_element_type=jnp.float32)


def dot_tn(a, b):
    return lax.dot_general(a, b, (((0,), (0,)), ((), ())), preferred_element_type=jnp.float32)


def relayout_kernel(in_ref, out_ref):
    for strip in range(STRIPS_PER_STEP):
        for k in range(PER_STRIP):
            start = (strip * PER_STRIP + k) * BLOCK
            out_ref[k, strip] = in_ref[:, start : start + BLOCK]


def relayout(rows):
    width = STRIPS_PER_STEP * PER_STRIP * BLOCK
    return pl.pallas_call(
        relayout_kernel,
        grid=(STRIPS // STRIPS_PER_STEP,),
        in_specs=[pl.BlockSpec((16, width), lambda i: (0, i))],
        out_specs=pl.BlockSpec((PER_STRIP, STRIPS_PER_STEP, 16, BLOCK), lambda i: (0, i, 0, 0)),
        out_shape=jax.ShapeDtypeStruct((PER_STRIP, STRIPS, 16, BLOCK), jnp.bfloat16),
    )(rows)


def gram_kernel(side_ref, in_ref, keep_ref, send_ref, mean_ref):
    side = side_ref[0]
    group = pl.program_id(0)
    block = in_ref[0]
    left = dot_nt(block, block)
    right = dot_tn(block, block)
    own = jnp.where(side == 0, left, right)
    other = jnp.where(side == 0, right, left)
    wide = block.astype(jnp.float32)

    @pl.when(group == 0)
    def _():
        keep_ref[...] = own
        send_ref[...] = other
        mean_ref[...] = wide

    @pl.when(group > 0)
    def _():
        keep_ref[...] += own
        send_ref[...] += other
        mean_ref[...] += wide


def grams(side, blocks):
    square = jax.ShapeDtypeStruct((BLOCK, BLOCK), jnp.float32)
    whole = pl.BlockSpec((BLOCK, BLOCK), lambda i: (0, 0))
    return pl.pallas_call(
        gram_kernel,
        grid=(blocks.shape[0],),
        in_specs=[
            pl.BlockSpec(memory_space=pltpu.SMEM),
            pl.BlockSpec((1, BLOCK, BLOCK), lambda i: (i, 0, 0)),
        ],
        out_specs=[whole, whole, whole],
        out_shape=[square, square, square],
        compiler_params=pltpu.CompilerParams(vmem_limit_bytes=32 * 1024 * 1024),
    )(side, blocks)


def root_kernel(own_ref, other_ref, out_ref):
    row = lax.broadcasted_iota(jnp.int32, (BLOCK, BLOCK), 0)
    col = lax.broadcasted_iota(jnp.int32, (BLOCK, BLOCK), 1)
    diagonal = row == col
    stat = own_ref[...] + other_ref[...]
    trace = jnp.sum(jnp.where(diagonal, stat, 0.0), keepdims=True)
    f = stat * (0.2 / trace)
    y = f
    for iteration in range(ITERS):
        fb = f.astype(jnp.bfloat16)
        if iteration > 0:
            y = y + f - dot_nn(y.astype(jnp.bfloat16), fb)
        if iteration + 1 < ITERS:
            g = 2.0 * f - dot_nn(fb, fb)
            gb = g.astype(jnp.bfloat16)
            h = 2.0 * g - dot_nn(gb, gb)
            f = 1.25**4 * (f - dot_nn(h.astype(jnp.bfloat16), fb))
    scale = lax.rsqrt(jnp.sqrt(trace * (1.0 / (GROUPS * BLOCK)))) * 1.25**ITERS
    out_ref[...] = (scale * (jnp.where(diagonal, 1.0, 0.0) - y)).astype(jnp.bfloat16)


def inverse_root(own, other):
    return pl.pallas_call(
        root_kernel,
        out_shape=jax.ShapeDtypeStruct((BLOCK, BLOCK), jnp.bfloat16),
        compiler_params=pltpu.CompilerParams(vmem_limit_bytes=48 * 1024 * 1024),
        cost_estimate=pl.CostEstimate(
            flops=20 * 2 * BLOCK**3, bytes_accessed=10 * BLOCK * BLOCK, transcendentals=0
        ),
    )(own, other)


def update_kernel(side_ref, own_ref, other_ref, mean_own_ref, mean_other_ref, out_ref):
    side = side_ref[0]
    mean = ((mean_own_ref[...] + mean_other_ref[...]) * (1.0 / GROUPS)).astype(jnp.bfloat16)

    def piece(left_ref, right_ref, start):
        inner = dot_nn(mean, right_ref[:, start : start + HALF]).astype(jnp.bfloat16)
        out_ref[...] = dot_nn(left_ref[...], inner).astype(jnp.bfloat16)

    @pl.when(side == 0)
    def _():
        piece(own_ref, other_ref, 0)

    @pl.when(side == 1)
    def _():
        piece(other_ref, own_ref, HALF)


def update_piece(side, own, other, mean_own, mean_other):
    vmem = pl.BlockSpec(memory_space=pltpu.VMEM)
    return pl.pallas_call(
        update_kernel,
        in_specs=[pl.BlockSpec(memory_space=pltpu.SMEM), vmem, vmem, vmem, vmem],
        out_shape=jax.ShapeDtypeStruct((BLOCK, HALF), jnp.bfloat16),
        compiler_params=pltpu.CompilerParams(vmem_limit_bytes=32 * 1024 * 1024),
    )(side, own, other, mean_own, mean_other)


def swap_cores(x):
    return lax.ppermute(x, "core", [(0, 1), (1, 0)])


def per_device(gradients):
    side = lax.axis_index("core").astype(jnp.int32).reshape(1)
    send = relayout(gradients[0]).reshape(PER_STRIP * STRIPS, 16, BLOCK)
    arrived = lax.all_to_all(send, ("x", "y", "z"), split_axis=0, concat_axis=0, tiled=True)
    blocks = arrived.reshape(PER_STRIP, BLOCK, BLOCK)
    keep, other, mean_own = grams(side, blocks)
    stat_other = swap_cores(other)
    mean_other = swap_cores(mean_own)
    own_root = inverse_root(keep, stat_other)
    other_root = swap_cores(own_root)
    piece = update_piece(side, own_root, other_root, mean_own, mean_other)
    return lax.all_to_all(
        piece.reshape(BLOCK, 1, 1, HALF), ("y", "z"), split_axis=0, concat_axis=1, tiled=True
    )


def solution(mesh):
    fine = Mesh(mesh.devices.reshape(4, 2, 4, 8), ("x", "core", "y", "z"))
    return jax.shard_map(
        per_device,
        mesh=fine,
        in_specs=(P(("x", "core"), ("y", "z"), None),),
        out_specs=P(("y", "z"), None, ("x", "core"), None),
        check_vma=False,
    )
```

```python
import jax
import jax.numpy as jnp
from jax import lax
from jax.experimental import pallas as pl
from jax.experimental.pallas import tpu as pltpu
from jax.sharding import Mesh
from jax.sharding import PartitionSpec as P

ITERS = 6
GROUPS = 8
BLOCK = 512
PER_STRIP = 4
STRIPS = 32
HALF = 256
CHUNKS = 8
CHUNK = 8192


def dot_nn(a, b):
    return lax.dot_general(a, b, (((1,), (0,)), ((), ())), preferred_element_type=jnp.float32)


def dot_nt(a, b):
    return lax.dot_general(a, b, (((1,), (1,)), ((), ())), preferred_element_type=jnp.float32)


def dot_tn(a, b):
    return lax.dot_general(a, b, (((0,), (0,)), ((), ())), preferred_element_type=jnp.float32)


def relayout_kernel(in_ref, out_ref, landed, sems):
    copies = []
    for chunk in range(CHUNKS):
        columns = pl.ds(chunk * CHUNK, CHUNK)
        copies.append(
            pltpu.make_async_copy(in_ref.at[:, columns], landed.at[:, columns], sems.at[chunk])
        )
        copies[-1].start()
    for chunk in range(CHUNKS):
        copies[chunk].wait()
        for index in range(chunk * CHUNK // BLOCK, (chunk + 1) * CHUNK // BLOCK):
            strip, k = divmod(index, PER_STRIP)
            out_ref[k * STRIPS + strip] = landed[:, index * BLOCK : (index + 1) * BLOCK]


def relayout(rows):
    return pl.pallas_call(
        relayout_kernel,
        in_specs=[pl.BlockSpec(memory_space=pltpu.HBM)],
        out_specs=pl.BlockSpec(memory_space=pltpu.VMEM),
        out_shape=jax.ShapeDtypeStruct((PER_STRIP * STRIPS, 16, BLOCK), jnp.bfloat16),
        scratch_shapes=[
            pltpu.VMEM((16, STRIPS * PER_STRIP * BLOCK), jnp.bfloat16),
            pltpu.SemaphoreType.DMA((CHUNKS,)),
        ],
        compiler_params=pltpu.CompilerParams(vmem_limit_bytes=16 * 1024 * 1024),
    )(rows)


def left_gram(in_ref):
    wide = jnp.concatenate([in_ref[g] for g in range(PER_STRIP)], axis=1)
    return dot_nt(wide, wide)


def right_gram(in_ref):
    tall = in_ref[...].reshape(PER_STRIP * BLOCK, BLOCK)
    return dot_tn(tall, tall)


def send_kernel(side_ref, in_ref, send_ref):
    @pl.when(side_ref[0] == 0)
    def _():
        send_ref[...] = right_gram(in_ref)

    @pl.when(side_ref[0] == 1)
    def _():
        send_ref[...] = left_gram(in_ref)


def keep_kernel(side_ref, in_ref, keep_ref, mean_ref):
    @pl.when(side_ref[0] == 0)
    def _():
        keep_ref[...] = left_gram(in_ref)

    @pl.when(side_ref[0] == 1)
    def _():
        keep_ref[...] = right_gram(in_ref)

    total = in_ref[0].astype(jnp.float32)
    for group in range(1, PER_STRIP):
        total += in_ref[group].astype(jnp.float32)
    mean_ref[...] = total


def gram(kernel, n_out, side, blocks):
    square = jax.ShapeDtypeStruct((BLOCK, BLOCK), jnp.float32)
    return pl.pallas_call(
        kernel,
        in_specs=[
            pl.BlockSpec(memory_space=pltpu.SMEM),
            pl.BlockSpec(memory_space=pltpu.VMEM),
        ],
        out_shape=[square] * n_out,
        compiler_params=pltpu.CompilerParams(vmem_limit_bytes=32 * 1024 * 1024),
        cost_estimate=pl.CostEstimate(
            flops=4 * 2 * BLOCK**3, bytes_accessed=16 * BLOCK * BLOCK, transcendentals=0
        ),
    )(side, blocks)


def root_kernel(own_ref, other_ref, out_ref):
    row = lax.broadcasted_iota(jnp.int32, (BLOCK, BLOCK), 0)
    col = lax.broadcasted_iota(jnp.int32, (BLOCK, BLOCK), 1)
    diagonal = row == col
    stat = own_ref[...] + other_ref[...]
    trace = jnp.sum(jnp.where(diagonal, stat, 0.0), keepdims=True)
    growth = 1.25**4
    f = stat * (0.2 / trace)
    y = None
    for iteration in range(ITERS - 1):
        fb = f.astype(jnp.bfloat16)
        f_squared = dot_nn(fb, fb)
        g = 2.0 * f - f_squared
        gb = g.astype(jnp.bfloat16)
        h = 2.0 * g - dot_nn(gb, gb)
        hb = h.astype(jnp.bfloat16)
        if iteration + 2 < ITERS:
            y = f if y is None else y + f - dot_nn(y.astype(jnp.bfloat16), fb)
            f = growth * (f - dot_nn(hb, fb))
        else:
            af = f - f_squared
            w = f + growth * (af - dot_nn(hb, af.astype(jnp.bfloat16)))
            y = y + w - dot_nn(y.astype(jnp.bfloat16), w.astype(jnp.bfloat16))
    scale = lax.rsqrt(jnp.sqrt(trace * (1.0 / (GROUPS * BLOCK)))) * 1.25**ITERS
    out_ref[...] = (scale * (jnp.where(diagonal, 1.0, 0.0) - y)).astype(jnp.bfloat16)


def inverse_root(own, other):
    return pl.pallas_call(
        root_kernel,
        out_shape=jax.ShapeDtypeStruct((BLOCK, BLOCK), jnp.bfloat16),
        compiler_params=pltpu.CompilerParams(vmem_limit_bytes=48 * 1024 * 1024),
        cost_estimate=pl.CostEstimate(
            flops=20 * 2 * BLOCK**3, bytes_accessed=10 * BLOCK * BLOCK, transcendentals=0
        ),
    )(own, other)


def update_kernel(side_ref, own_ref, other_ref, mean_own_ref, mean_other_ref, out_ref):
    side = side_ref[0]
    mean = ((mean_own_ref[...] + mean_other_ref[...]) * (1.0 / GROUPS)).astype(jnp.bfloat16)

    def piece(left_ref, right_ref, start):
        inner = dot_nn(mean, right_ref[:, start : start + HALF]).astype(jnp.bfloat16)
        out_ref[...] = dot_nn(left_ref[...], inner).astype(jnp.bfloat16)

    @pl.when(side == 0)
    def _():
        piece(own_ref, other_ref, 0)

    @pl.when(side == 1)
    def _():
        piece(other_ref, own_ref, HALF)


def update_piece(side, own, other, mean_own, mean_other):
    vmem = pl.BlockSpec(memory_space=pltpu.VMEM)
    return pl.pallas_call(
        update_kernel,
        in_specs=[pl.BlockSpec(memory_space=pltpu.SMEM), vmem, vmem, vmem, vmem],
        out_shape=jax.ShapeDtypeStruct((BLOCK, HALF), jnp.bfloat16),
        compiler_params=pltpu.CompilerParams(vmem_limit_bytes=32 * 1024 * 1024),
    )(side, own, other, mean_own, mean_other)


def swap_cores(x):
    return lax.ppermute(x, "core", [(0, 1), (1, 0)])


def per_device(gradients):
    side = lax.axis_index("core").astype(jnp.int32).reshape(1)
    send = relayout(gradients[0])
    arrived = lax.all_to_all(send, ("x", "y", "z"), split_axis=0, concat_axis=0, tiled=True)
    blocks = arrived.reshape(PER_STRIP, BLOCK, BLOCK)
    (other,) = gram(send_kernel, 1, side, blocks)
    stat_other = swap_cores(other)
    keep, mean_own = gram(keep_kernel, 2, side, blocks)
    mean_other = swap_cores(mean_own)
    own_root = inverse_root(keep, stat_other)
    other_root = swap_cores(own_root)
    piece = update_piece(side, own_root, other_root, mean_own, mean_other)
    rows = lax.all_to_all(
        piece.reshape(STRIPS, 16, HALF), ("y", "z"), split_axis=0, concat_axis=0, tiled=True
    )
    return jnp.swapaxes(rows, 0, 1)[:, :, None, :]


def solution(mesh):
    fine = Mesh(mesh.devices.reshape(4, 2, 4, 8), ("x", "core", "y", "z"))
    return jax.shard_map(
        per_device,
        mesh=fine,
        in_specs=(P(("x", "core"), ("y", "z"), None),),
        out_specs=P(("y", "z"), None, ("x", "core"), None),
        check_vma=False,
    )
```

```python
import jax
import jax.numpy as jnp
from jax import lax
from jax.experimental import pallas as pl
from jax.experimental.pallas import tpu as pltpu
from jax.sharding import Mesh
from jax.sharding import PartitionSpec as P

ITERS = 6
GROUPS = 8
BLOCK = 512
PER_STRIP = 4
STRIPS = 32
HALF = 256
CHUNKS = 8
CHUNK = 8192


def dot_nn(a, b):
    return lax.dot_general(a, b, (((1,), (0,)), ((), ())), preferred_element_type=jnp.float32)


def dot_nt(a, b):
    return lax.dot_general(a, b, (((1,), (1,)), ((), ())), preferred_element_type=jnp.float32)


def dot_tn(a, b):
    return lax.dot_general(a, b, (((0,), (0,)), ((), ())), preferred_element_type=jnp.float32)


def relayout_kernel(in_ref, out_ref, landed, sems):
    copies = []
    for chunk in range(CHUNKS):
        columns = pl.ds(chunk * CHUNK, CHUNK)
        copies.append(
            pltpu.make_async_copy(in_ref.at[:, columns], landed.at[:, columns], sems.at[chunk])
        )
        copies[-1].start()
    for chunk in range(CHUNKS):
        copies[chunk].wait()
        for index in range(chunk * CHUNK // BLOCK, (chunk + 1) * CHUNK // BLOCK):
            strip, k = divmod(index, PER_STRIP)
            out_ref[k * STRIPS + strip] = landed[:, index * BLOCK : (index + 1) * BLOCK]


def relayout(rows):
    return pl.pallas_call(
        relayout_kernel,
        in_specs=[pl.BlockSpec(memory_space=pl.ANY)],
        out_specs=pl.BlockSpec(memory_space=pltpu.VMEM),
        out_shape=jax.ShapeDtypeStruct((PER_STRIP * STRIPS, 16, BLOCK), jnp.bfloat16),
        scratch_shapes=[
            pltpu.VMEM((16, STRIPS * PER_STRIP * BLOCK), jnp.bfloat16),
            pltpu.SemaphoreType.DMA((CHUNKS,)),
        ],
        compiler_params=pltpu.CompilerParams(vmem_limit_bytes=50 * 1024 * 1024),
    )(rows)


def left_gram(in_ref):
    wide = jnp.concatenate([in_ref[g] for g in range(PER_STRIP)], axis=1)
    return dot_nt(wide, wide)


def right_gram(in_ref):
    tall = in_ref[...].reshape(PER_STRIP * BLOCK, BLOCK)
    return dot_tn(tall, tall)


def send_kernel(side_ref, in_ref, send_ref):
    @pl.when(side_ref[0] == 0)
    def _():
        send_ref[...] = right_gram(in_ref)

    @pl.when(side_ref[0] == 1)
    def _():
        send_ref[...] = left_gram(in_ref)


def keep_kernel(side_ref, in_ref, keep_ref, mean_ref):
    @pl.when(side_ref[0] == 0)
    def _():
        keep_ref[...] = left_gram(in_ref)

    @pl.when(side_ref[0] == 1)
    def _():
        keep_ref[...] = right_gram(in_ref)

    total = in_ref[0].astype(jnp.float32)
    for group in range(1, PER_STRIP):
        total += in_ref[group].astype(jnp.float32)
    mean_ref[...] = total


def gram(kernel, n_out, side, blocks):
    square = jax.ShapeDtypeStruct((BLOCK, BLOCK), jnp.float32)
    return pl.pallas_call(
        kernel,
        in_specs=[
            pl.BlockSpec(memory_space=pltpu.SMEM),
            pl.BlockSpec(memory_space=pltpu.VMEM),
        ],
        out_shape=[square] * n_out,
        compiler_params=pltpu.CompilerParams(vmem_limit_bytes=32 * 1024 * 1024),
        cost_estimate=pl.CostEstimate(
            flops=4 * 2 * BLOCK**3, bytes_accessed=16 * BLOCK * BLOCK, transcendentals=0
        ),
    )(side, blocks)


def root_kernel(own_ref, other_ref, out_ref):
    row = lax.broadcasted_iota(jnp.int32, (BLOCK, BLOCK), 0)
    col = lax.broadcasted_iota(jnp.int32, (BLOCK, BLOCK), 1)
    diagonal = row == col
    stat = own_ref[...] + other_ref[...]
    trace = jnp.sum(jnp.where(diagonal, stat, 0.0), keepdims=True)
    growth = 1.25**4
    f = stat * (0.2 / trace)
    y = None
    for iteration in range(ITERS - 1):
        fb = f.astype(jnp.bfloat16)
        f_squared = dot_nn(fb, fb)
        g = 2.0 * f - f_squared
        gb = g.astype(jnp.bfloat16)
        h = 2.0 * g - dot_nn(gb, gb)
        hb = h.astype(jnp.bfloat16)
        if iteration + 2 < ITERS:
            y = f if y is None else y + f - dot_nn(y.astype(jnp.bfloat16), fb)
            f = growth * (f - dot_nn(hb, fb))
        else:
            af = f - f_squared
            w = f + growth * (af - dot_nn(hb, af.astype(jnp.bfloat16)))
            y = y + w - dot_nn(y.astype(jnp.bfloat16), w.astype(jnp.bfloat16))
    scale = lax.rsqrt(jnp.sqrt(trace * (1.0 / (GROUPS * BLOCK)))) * 1.25**ITERS
    out_ref[...] = (scale * (jnp.where(diagonal, 1.0, 0.0) - y)).astype(jnp.bfloat16)


def inverse_root(own, other):
    return pl.pallas_call(
        root_kernel,
        out_shape=jax.ShapeDtypeStruct((BLOCK, BLOCK), jnp.bfloat16),
        compiler_params=pltpu.CompilerParams(vmem_limit_bytes=48 * 1024 * 1024),
        cost_estimate=pl.CostEstimate(
            flops=20 * 2 * BLOCK**3, bytes_accessed=10 * BLOCK * BLOCK, transcendentals=0
        ),
    )(own, other)


def update_kernel(side_ref, own_ref, other_ref, mean_own_ref, mean_other_ref, out_ref):
    side = side_ref[0]
    mean = ((mean_own_ref[...] + mean_other_ref[...]) * (1.0 / GROUPS)).astype(jnp.bfloat16)

    def piece(left_ref, right_ref, start):
        inner = dot_nn(mean, right_ref[:, start : start + HALF]).astype(jnp.bfloat16)
        out_ref[...] = dot_nn(left_ref[...], inner).astype(jnp.bfloat16)

    @pl.when(side == 0)
    def _():
        piece(own_ref, other_ref, 0)

    @pl.when(side == 1)
    def _():
        piece(other_ref, own_ref, HALF)


def update_piece(side, own, other, mean_own, mean_other):
    vmem = pl.BlockSpec(memory_space=pltpu.VMEM)
    return pl.pallas_call(
        update_kernel,
        in_specs=[pl.BlockSpec(memory_space=pltpu.SMEM), vmem, vmem, vmem, vmem],
        out_shape=jax.ShapeDtypeStruct((BLOCK, HALF), jnp.bfloat16),
        compiler_params=pltpu.CompilerParams(vmem_limit_bytes=32 * 1024 * 1024),
    )(side, own, other, mean_own, mean_other)


def swap_cores(x):
    return lax.ppermute(x, "core", [(0, 1), (1, 0)])


def per_device(gradients):
    side = lax.axis_index("core").astype(jnp.int32).reshape(1)
    send = relayout(gradients[0])
    arrived = lax.all_to_all(send, ("x", "y", "z"), split_axis=0, concat_axis=0, tiled=True)
    blocks = arrived.reshape(PER_STRIP, BLOCK, BLOCK)
    (other,) = gram(send_kernel, 1, side, blocks)
    stat_other = swap_cores(other)
    keep, mean_own = gram(keep_kernel, 2, side, blocks)
    mean_other = swap_cores(mean_own)
    own_root = inverse_root(keep, stat_other)
    other_root = swap_cores(own_root)
    piece = update_piece(side, own_root, other_root, mean_own, mean_other)
    rows = lax.all_to_all(
        piece.reshape(STRIPS, 16, HALF), ("y", "z"), split_axis=0, concat_axis=0, tiled=True
    )
    return jnp.swapaxes(rows, 0, 1)[:, :, None, :]


def solution(mesh):
    fine = Mesh(mesh.devices.reshape(4, 2, 4, 8), ("x", "core", "y", "z"))
    return jax.shard_map(
        per_device,
        mesh=fine,
        in_specs=(P(("x", "core"), ("y", "z"), None),),
        out_specs=P(("y", "z"), None, ("x", "core"), None),
        check_vma=False,
    )
```

```python
import jax
import jax.numpy as jnp
from jax import lax
from jax.experimental import pallas as pl
from jax.experimental.pallas import tpu as pltpu
from jax.sharding import Mesh
from jax.sharding import PartitionSpec as P

ITERS = 6
GROUPS = 8
BLOCK = 512
PER_STRIP = 4
STRIPS = 32
HALF = 256
CHUNKS = 8
CHUNK = 8192


def dot_nn(a, b):
    return lax.dot_general(a, b, (((1,), (0,)), ((), ())), preferred_element_type=jnp.float32)


def dot_nt(a, b):
    return lax.dot_general(a, b, (((1,), (1,)), ((), ())), preferred_element_type=jnp.float32)


def dot_tn(a, b):
    return lax.dot_general(a, b, (((0,), (0,)), ((), ())), preferred_element_type=jnp.float32)


def relayout_kernel(in_ref, out_ref, landed, sems):
    copies = []
    for chunk in range(CHUNKS):
        columns = pl.ds(chunk * CHUNK, CHUNK)
        copies.append(
            pltpu.make_async_copy(in_ref.at[:, columns], landed.at[:, columns], sems.at[chunk])
        )
        copies[-1].start()
    for chunk in range(CHUNKS):
        copies[chunk].wait()
        for index in range(chunk * CHUNK // BLOCK, (chunk + 1) * CHUNK // BLOCK):
            strip, k = divmod(index, PER_STRIP)
            out_ref[k * STRIPS + strip] = landed[:, index * BLOCK : (index + 1) * BLOCK]


def relayout(rows):
    return pl.pallas_call(
        relayout_kernel,
        in_specs=[pl.BlockSpec(memory_space=pl.ANY)],
        out_specs=pl.BlockSpec(memory_space=pltpu.VMEM),
        out_shape=jax.ShapeDtypeStruct((PER_STRIP * STRIPS, 16, BLOCK), jnp.bfloat16),
        scratch_shapes=[
            pltpu.VMEM((16, STRIPS * PER_STRIP * BLOCK), jnp.bfloat16),
            pltpu.SemaphoreType.DMA((CHUNKS,)),
        ],
        compiler_params=pltpu.CompilerParams(vmem_limit_bytes=50 * 1024 * 1024),
    )(rows)


def left_gram(in_ref):
    wide = jnp.concatenate([in_ref[g] for g in range(PER_STRIP)], axis=1)
    return dot_nt(wide, wide)


def right_gram(in_ref):
    tall = in_ref[...].reshape(PER_STRIP * BLOCK, BLOCK)
    return dot_tn(tall, tall)


def send_kernel(in_ref, send_ref):
    side = lax.axis_index("core")

    @pl.when(side == 0)
    def _():
        send_ref[...] = right_gram(in_ref)

    @pl.when(side == 1)
    def _():
        send_ref[...] = left_gram(in_ref)


def keep_kernel(in_ref, keep_ref, mean_ref):
    side = lax.axis_index("core")

    @pl.when(side == 0)
    def _():
        keep_ref[...] = left_gram(in_ref)

    @pl.when(side == 1)
    def _():
        keep_ref[...] = right_gram(in_ref)

    total = in_ref[0].astype(jnp.float32)
    for group in range(1, PER_STRIP):
        total += in_ref[group].astype(jnp.float32)
    mean_ref[...] = total


def gram(kernel, n_out, blocks):
    square = jax.ShapeDtypeStruct((BLOCK, BLOCK), jnp.float32)
    return pl.pallas_call(
        kernel,
        out_shape=[square] * n_out,
        compiler_params=pltpu.CompilerParams(vmem_limit_bytes=32 * 1024 * 1024),
        cost_estimate=pl.CostEstimate(
            flops=4 * 2 * BLOCK**3, bytes_accessed=16 * BLOCK * BLOCK, transcendentals=0
        ),
    )(blocks)


def root_kernel(own_ref, other_ref, out_ref):
    row = lax.broadcasted_iota(jnp.int32, (BLOCK, BLOCK), 0)
    col = lax.broadcasted_iota(jnp.int32, (BLOCK, BLOCK), 1)
    diagonal = row == col
    stat = own_ref[...] + other_ref[...]
    trace = jnp.sum(jnp.where(diagonal, stat, 0.0), keepdims=True)
    growth = 1.25**4
    f = stat * (0.2 / trace)
    y = None
    for iteration in range(ITERS - 1):
        fb = f.astype(jnp.bfloat16)
        f_squared = dot_nn(fb, fb)
        g = 2.0 * f - f_squared
        gb = g.astype(jnp.bfloat16)
        h = 2.0 * g - dot_nn(gb, gb)
        hb = h.astype(jnp.bfloat16)
        if iteration + 2 < ITERS:
            y = f if y is None else y + f - dot_nn(y.astype(jnp.bfloat16), fb)
            f = growth * (f - dot_nn(hb, fb))
        else:
            af = f - f_squared
            w = f + growth * (af - dot_nn(hb, af.astype(jnp.bfloat16)))
            y = y + w - dot_nn(y.astype(jnp.bfloat16), w.astype(jnp.bfloat16))
    scale = lax.rsqrt(jnp.sqrt(trace * (1.0 / (GROUPS * BLOCK)))) * 1.25**ITERS
    out_ref[...] = (scale * (jnp.where(diagonal, 1.0, 0.0) - y)).astype(jnp.bfloat16)


def inverse_root(own, other):
    return pl.pallas_call(
        root_kernel,
        out_shape=jax.ShapeDtypeStruct((BLOCK, BLOCK), jnp.bfloat16),
        compiler_params=pltpu.CompilerParams(vmem_limit_bytes=48 * 1024 * 1024),
        cost_estimate=pl.CostEstimate(
            flops=20 * 2 * BLOCK**3, bytes_accessed=10 * BLOCK * BLOCK, transcendentals=0
        ),
    )(own, other)


def update_kernel(own_ref, other_ref, mean_own_ref, mean_other_ref, out_ref):
    side = lax.axis_index("core")
    mean = ((mean_own_ref[...] + mean_other_ref[...]) * (1.0 / GROUPS)).astype(jnp.bfloat16)

    def piece(left_ref, right_ref, start):
        inner = dot_nn(mean, right_ref[:, start : start + HALF]).astype(jnp.bfloat16)
        out_ref[...] = dot_nn(left_ref[...], inner).astype(jnp.bfloat16)

    @pl.when(side == 0)
    def _():
        piece(own_ref, other_ref, 0)

    @pl.when(side == 1)
    def _():
        piece(other_ref, own_ref, HALF)


def update_piece(own, other, mean_own, mean_other):
    return pl.pallas_call(
        update_kernel,
        out_shape=jax.ShapeDtypeStruct((BLOCK, HALF), jnp.bfloat16),
        compiler_params=pltpu.CompilerParams(vmem_limit_bytes=32 * 1024 * 1024),
    )(own, other, mean_own, mean_other)


def swap_cores(x):
    return lax.ppermute(x, "core", [(0, 1), (1, 0)])


def per_device(gradients):
    send = relayout(gradients[0])
    arrived = lax.all_to_all(send, ("x", "y", "z"), split_axis=0, concat_axis=0, tiled=True)
    blocks = arrived.reshape(PER_STRIP, BLOCK, BLOCK)
    (other,) = gram(send_kernel, 1, blocks)
    stat_other = swap_cores(other)
    keep, mean_own = gram(keep_kernel, 2, blocks)
    mean_other = swap_cores(mean_own)
    own_root = inverse_root(keep, stat_other)
    other_root = swap_cores(own_root)
    piece = update_piece(own_root, other_root, mean_own, mean_other)
    rows = lax.all_to_all(
        piece.reshape(STRIPS, 16, HALF), ("y", "z"), split_axis=0, concat_axis=0, tiled=True
    )
    return jnp.swapaxes(rows, 0, 1)[:, :, None, :]


def solution(mesh):
    fine = Mesh(mesh.devices.reshape(4, 2, 4, 8), ("x", "core", "y", "z"))
    return jax.shard_map(
        per_device,
        mesh=fine,
        in_specs=(P(("x", "core"), ("y", "z"), None),),
        out_specs=P(("y", "z"), None, ("x", "core"), None),
        check_vma=False,
    )
```

```python
import jax
import jax.numpy as jnp
from jax import lax
from jax.experimental import pallas as pl
from jax.experimental.pallas import tpu as pltpu
from jax.sharding import Mesh
from jax.sharding import PartitionSpec as P

ITERS = 6
GROUPS = 8
BLOCK = 512
PER_STRIP = 4
STRIPS = 32
HALF = 256
QUARTER = 128
CHUNKS = 8
CHUNK = 8192


def dot_nn(a, b):
    return lax.dot_general(a, b, (((1,), (0,)), ((), ())), preferred_element_type=jnp.float32)


def dot_nt(a, b):
    return lax.dot_general(a, b, (((1,), (1,)), ((), ())), preferred_element_type=jnp.float32)


def dot_tn(a, b):
    return lax.dot_general(a, b, (((0,), (0,)), ((), ())), preferred_element_type=jnp.float32)


def relayout_kernel(in_ref, out_ref, landed, sems):
    copies = []
    for chunk in range(CHUNKS):
        columns = pl.ds(chunk * CHUNK, CHUNK)
        copies.append(
            pltpu.make_async_copy(in_ref.at[:, columns], landed.at[:, columns], sems.at[chunk])
        )
        copies[-1].start()
    for chunk in range(CHUNKS):
        copies[chunk].wait()
        for index in range(chunk * CHUNK // BLOCK, (chunk + 1) * CHUNK // BLOCK):
            strip, k = divmod(index, PER_STRIP)
            out_ref[k * STRIPS + strip] = landed[:, index * BLOCK : (index + 1) * BLOCK]


def relayout(rows):
    return pl.pallas_call(
        relayout_kernel,
        in_specs=[pl.BlockSpec(memory_space=pl.ANY)],
        out_specs=pl.BlockSpec(memory_space=pltpu.VMEM),
        out_shape=jax.ShapeDtypeStruct((PER_STRIP * STRIPS, 16, BLOCK), jnp.bfloat16),
        scratch_shapes=[
            pltpu.VMEM((16, STRIPS * PER_STRIP * BLOCK), jnp.bfloat16),
            pltpu.SemaphoreType.DMA((CHUNKS,)),
        ],
        compiler_params=pltpu.CompilerParams(vmem_limit_bytes=50 * 1024 * 1024),
    )(rows)


def left_gram(in_ref, out_ref):
    wide = jnp.concatenate([in_ref[g] for g in range(PER_STRIP)], axis=1)
    low = wide[HALF:]
    store_gram(dot_nt(wide[:HALF], wide), dot_nt(low, low), out_ref)


def right_gram(in_ref, out_ref):
    tall = in_ref[...].reshape(PER_STRIP * BLOCK, BLOCK)
    low = tall[:, HALF:]
    store_gram(dot_tn(tall[:, :HALF], tall), dot_tn(low, low), out_ref)


def store_gram(top, corner, out_ref):
    out_ref[:HALF] = top
    out_ref[HALF:, :HALF] = corner[:QUARTER]
    out_ref[HALF:, HALF:] = corner[QUARTER:]


def send_kernel(in_ref, send_ref):
    side = lax.axis_index("core")

    @pl.when(side == 0)
    def _():
        right_gram(in_ref, send_ref)

    @pl.when(side == 1)
    def _():
        left_gram(in_ref, send_ref)


def keep_kernel(in_ref, keep_ref, mean_ref):
    side = lax.axis_index("core")

    @pl.when(side == 0)
    def _():
        left_gram(in_ref, keep_ref)

    @pl.when(side == 1)
    def _():
        right_gram(in_ref, keep_ref)

    total = in_ref[0].astype(jnp.float32)
    for group in range(1, PER_STRIP):
        total += in_ref[group].astype(jnp.float32)
    mean_ref[...] = total


def gram(kernel, rows, blocks):
    return pl.pallas_call(
        kernel,
        out_shape=[jax.ShapeDtypeStruct((n, BLOCK), jnp.float32) for n in rows],
        compiler_params=pltpu.CompilerParams(vmem_limit_bytes=32 * 1024 * 1024),
        cost_estimate=pl.CostEstimate(
            flops=4 * 2 * BLOCK**3, bytes_accessed=16 * BLOCK * BLOCK, transcendentals=0
        ),
    )(blocks)


def root_kernel(own_ref, other_ref, out_ref):
    row = lax.broadcasted_iota(jnp.int32, (BLOCK, BLOCK), 0)
    col = lax.broadcasted_iota(jnp.int32, (BLOCK, BLOCK), 1)
    diagonal = row == col
    packed = own_ref[...] + other_ref[...]
    low = jnp.concatenate([packed[HALF:, :HALF], packed[HALF:, HALF:]], axis=0)
    low = jnp.concatenate([packed[:HALF, HALF:].T, low], axis=1)
    stat = jnp.concatenate([packed[:HALF], low], axis=0)
    trace = jnp.sum(jnp.where(diagonal, stat, 0.0), keepdims=True)
    growth = 1.25**4
    f = stat * (0.2 / trace)
    y = None
    for iteration in range(ITERS - 1):
        fb = f.astype(jnp.bfloat16)
        f_squared = dot_nn(fb, fb)
        g = 2.0 * f - f_squared
        gb = g.astype(jnp.bfloat16)
        h = 2.0 * g - dot_nn(gb, gb)
        hb = h.astype(jnp.bfloat16)
        if iteration + 2 < ITERS:
            y = f if y is None else y + f - dot_nn(y.astype(jnp.bfloat16), fb)
            f = growth * (f - dot_nn(hb, fb))
        else:
            af = f - f_squared
            w = f + growth * (af - dot_nn(hb, af.astype(jnp.bfloat16)))
            y = y + w - dot_nn(y.astype(jnp.bfloat16), w.astype(jnp.bfloat16))
    scale = lax.rsqrt(jnp.sqrt(trace * (1.0 / (GROUPS * BLOCK)))) * 1.25**ITERS
    out_ref[...] = (scale * (jnp.where(diagonal, 1.0, 0.0) - y)).astype(jnp.bfloat16)


def inverse_root(own, other):
    return pl.pallas_call(
        root_kernel,
        out_shape=jax.ShapeDtypeStruct((BLOCK, BLOCK), jnp.bfloat16),
        compiler_params=pltpu.CompilerParams(vmem_limit_bytes=48 * 1024 * 1024),
        cost_estimate=pl.CostEstimate(
            flops=20 * 2 * BLOCK**3, bytes_accessed=10 * BLOCK * BLOCK, transcendentals=0
        ),
    )(own, other)


def mean_kernel(own_ref, other_ref, out_ref):
    out_ref[...] = ((own_ref[...] + other_ref[...]) * (1.0 / GROUPS)).astype(jnp.bfloat16)


def mean_block(own, other):
    return pl.pallas_call(
        mean_kernel,
        out_shape=jax.ShapeDtypeStruct((BLOCK, BLOCK), jnp.bfloat16),
        compiler_params=pltpu.CompilerParams(vmem_limit_bytes=16 * 1024 * 1024),
        cost_estimate=pl.CostEstimate(
            flops=2 * BLOCK * BLOCK, bytes_accessed=10 * BLOCK * BLOCK, transcendentals=0
        ),
    )(own, other)


def update_kernel(own_ref, other_ref, mean_ref, out_ref):
    side = lax.axis_index("core")

    def piece(left_ref, right_ref, start):
        right = right_ref[:, start : start + HALF]
        inner = dot_nn(mean_ref[...], right).astype(jnp.bfloat16)
        out_ref[...] = dot_nn(left_ref[...], inner).astype(jnp.bfloat16)

    @pl.when(side == 0)
    def _():
        piece(own_ref, other_ref, 0)

    @pl.when(side == 1)
    def _():
        piece(other_ref, own_ref, HALF)


def update_piece(own, other, mean):
    return pl.pallas_call(
        update_kernel,
        out_shape=jax.ShapeDtypeStruct((BLOCK, HALF), jnp.bfloat16),
        compiler_params=pltpu.CompilerParams(vmem_limit_bytes=32 * 1024 * 1024),
    )(own, other, mean)


def swap_cores(x):
    return lax.ppermute(x, "core", [(0, 1), (1, 0)])


def per_device(gradients):
    send = relayout(gradients[0])
    arrived = lax.all_to_all(send, ("x", "y", "z"), split_axis=0, concat_axis=0, tiled=True)
    blocks = arrived.reshape(PER_STRIP, BLOCK, BLOCK)
    (other,) = gram(send_kernel, (HALF + QUARTER,), blocks)
    stat_other = swap_cores(other)
    keep, mean_own = gram(keep_kernel, (HALF + QUARTER, BLOCK), blocks)
    mean_other = swap_cores(mean_own)
    own_root = inverse_root(keep, stat_other)
    other_root = swap_cores(own_root)
    piece = update_piece(own_root, other_root, mean_block(mean_own, mean_other))
    rows = lax.all_to_all(
        piece.reshape(STRIPS, 16, HALF), ("y", "z"), split_axis=0, concat_axis=0, tiled=True
    )
    return jnp.swapaxes(rows, 0, 1)[:, :, None, :]


def solution(mesh):
    fine = Mesh(mesh.devices.reshape(4, 2, 4, 8), ("x", "core", "y", "z"))
    return jax.shard_map(
        per_device,
        mesh=fine,
        in_specs=(P(("x", "core"), ("y", "z"), None),),
        out_specs=P(("y", "z"), None, ("x", "core"), None),
        check_vma=False,
    )
```

```python
import jax
import jax.numpy as jnp
from jax import lax
from jax.experimental import pallas as pl
from jax.experimental.pallas import tpu as pltpu
from jax.sharding import Mesh
from jax.sharding import PartitionSpec as P

ITERS = 6
GROUPS = 8
BLOCK = 512
PER_STRIP = 4
STRIPS = 32
HALF = 256
QUARTER = 128
CHUNKS = 8
CHUNK = 8192


def dot_nn(a, b):
    return lax.dot_general(a, b, (((1,), (0,)), ((), ())), preferred_element_type=jnp.float32)


def dot_nt(a, b):
    return lax.dot_general(a, b, (((1,), (1,)), ((), ())), preferred_element_type=jnp.float32)


def dot_tn(a, b):
    return lax.dot_general(a, b, (((0,), (0,)), ((), ())), preferred_element_type=jnp.float32)


def split_product(a, b):
    a_high, b_high = a.astype(jnp.bfloat16), b.astype(jnp.bfloat16)
    a_low = (a - a_high.astype(jnp.float32)).astype(jnp.bfloat16)
    b_low = (b - b_high.astype(jnp.float32)).astype(jnp.bfloat16)
    return dot_nn(
        jnp.concatenate([a_high, a_high, a_low], axis=1),
        jnp.concatenate([b_high, b_low, b_high], axis=0),
    )


def relayout_kernel(in_ref, out_ref, landed, sems):
    copies = []
    for chunk in range(CHUNKS):
        columns = pl.ds(chunk * CHUNK, CHUNK)
        copies.append(
            pltpu.make_async_copy(in_ref.at[:, columns], landed.at[:, columns], sems.at[chunk])
        )
        copies[-1].start()
    for chunk in range(CHUNKS):
        copies[chunk].wait()
        for index in range(chunk * CHUNK // BLOCK, (chunk + 1) * CHUNK // BLOCK):
            strip, k = divmod(index, PER_STRIP)
            out_ref[k * STRIPS + strip] = landed[:, index * BLOCK : (index + 1) * BLOCK]


def relayout(rows):
    return pl.pallas_call(
        relayout_kernel,
        in_specs=[pl.BlockSpec(memory_space=pl.ANY)],
        out_specs=pl.BlockSpec(memory_space=pltpu.VMEM),
        out_shape=jax.ShapeDtypeStruct((PER_STRIP * STRIPS, 16, BLOCK), jnp.bfloat16),
        scratch_shapes=[
            pltpu.VMEM((16, STRIPS * PER_STRIP * BLOCK), jnp.bfloat16),
            pltpu.SemaphoreType.DMA((CHUNKS,)),
        ],
        compiler_params=pltpu.CompilerParams(vmem_limit_bytes=50 * 1024 * 1024),
    )(rows)


def left_gram(in_ref, out_ref):
    wide = jnp.concatenate([in_ref[g] for g in range(PER_STRIP)], axis=1)
    low = wide[HALF:]
    store_gram(dot_nt(wide[:HALF], wide), dot_nt(low, low), out_ref)


def right_gram(in_ref, out_ref):
    tall = in_ref[...].reshape(PER_STRIP * BLOCK, BLOCK)
    low = tall[:, HALF:]
    store_gram(dot_tn(tall[:, :HALF], tall), dot_tn(low, low), out_ref)


def store_gram(top, corner, out_ref):
    out_ref[:HALF] = top
    out_ref[HALF:, :HALF] = corner[:QUARTER]
    out_ref[HALF:, HALF:] = corner[QUARTER:]


def send_kernel(in_ref, send_ref):
    side = lax.axis_index("core")

    @pl.when(side == 0)
    def _():
        right_gram(in_ref, send_ref)

    @pl.when(side == 1)
    def _():
        left_gram(in_ref, send_ref)


def keep_kernel(in_ref, keep_ref, mean_ref):
    side = lax.axis_index("core")

    @pl.when(side == 0)
    def _():
        left_gram(in_ref, keep_ref)

    @pl.when(side == 1)
    def _():
        right_gram(in_ref, keep_ref)

    total = in_ref[0].astype(jnp.float32)
    for group in range(1, PER_STRIP):
        total += in_ref[group].astype(jnp.float32)
    mean_ref[...] = total


def gram(kernel, rows, blocks):
    return pl.pallas_call(
        kernel,
        out_shape=[jax.ShapeDtypeStruct((n, BLOCK), jnp.float32) for n in rows],
        compiler_params=pltpu.CompilerParams(vmem_limit_bytes=32 * 1024 * 1024),
        cost_estimate=pl.CostEstimate(
            flops=4 * 2 * BLOCK**3, bytes_accessed=16 * BLOCK * BLOCK, transcendentals=0
        ),
    )(blocks)


def root_kernel(own_ref, other_ref, out_ref):
    row = lax.broadcasted_iota(jnp.int32, (BLOCK, BLOCK), 0)
    col = lax.broadcasted_iota(jnp.int32, (BLOCK, BLOCK), 1)
    diagonal = row == col
    packed = own_ref[...] + other_ref[...]
    low = jnp.concatenate([packed[HALF:, :HALF], packed[HALF:, HALF:]], axis=0)
    low = jnp.concatenate([packed[:HALF, HALF:].T, low], axis=1)
    stat = jnp.concatenate([packed[:HALF], low], axis=0)
    trace = jnp.sum(jnp.where(diagonal, stat, 0.0), keepdims=True)
    growth = 1.25**4
    f = stat * (0.2 / trace)
    y = None
    for iteration in range(ITERS - 1):
        fb = f.astype(jnp.bfloat16)
        f_squared = dot_nn(fb, fb)
        g = 2.0 * f - f_squared
        gb = g.astype(jnp.bfloat16)
        h = 2.0 * g - dot_nn(gb, gb)
        hb = h.astype(jnp.bfloat16)
        if iteration + 2 < ITERS:
            y = f if y is None else y + f - dot_nn(y.astype(jnp.bfloat16), fb)
            hf = split_product(h, f) if iteration < 2 else dot_nn(hb, fb)
            f = growth * (f - hf)
        else:
            af = f - f_squared
            w = f + growth * (af - dot_nn(hb, af.astype(jnp.bfloat16)))
            y = y + w - dot_nn(y.astype(jnp.bfloat16), w.astype(jnp.bfloat16))
    scale = lax.rsqrt(jnp.sqrt(trace * (1.0 / (GROUPS * BLOCK)))) * 1.25**ITERS
    out_ref[...] = (scale * (jnp.where(diagonal, 1.0, 0.0) - y)).astype(jnp.bfloat16)


def inverse_root(own, other):
    return pl.pallas_call(
        root_kernel,
        out_shape=jax.ShapeDtypeStruct((BLOCK, BLOCK), jnp.bfloat16),
        compiler_params=pltpu.CompilerParams(vmem_limit_bytes=48 * 1024 * 1024),
        cost_estimate=pl.CostEstimate(
            flops=20 * 2 * BLOCK**3, bytes_accessed=10 * BLOCK * BLOCK, transcendentals=0
        ),
    )(own, other)


def mean_kernel(own_ref, other_ref, out_ref):
    out_ref[...] = ((own_ref[...] + other_ref[...]) * (1.0 / GROUPS)).astype(jnp.bfloat16)


def mean_block(own, other):
    return pl.pallas_call(
        mean_kernel,
        out_shape=jax.ShapeDtypeStruct((BLOCK, BLOCK), jnp.bfloat16),
        compiler_params=pltpu.CompilerParams(vmem_limit_bytes=16 * 1024 * 1024),
        cost_estimate=pl.CostEstimate(
            flops=2 * BLOCK * BLOCK, bytes_accessed=10 * BLOCK * BLOCK, transcendentals=0
        ),
    )(own, other)


def update_kernel(own_ref, other_ref, mean_ref, out_ref):
    side = lax.axis_index("core")

    def piece(left_ref, right_ref, start):
        right = right_ref[:, start : start + HALF]
        inner = dot_nn(mean_ref[...], right).astype(jnp.bfloat16)
        out_ref[...] = dot_nn(left_ref[...], inner).astype(jnp.bfloat16)

    @pl.when(side == 0)
    def _():
        piece(own_ref, other_ref, 0)

    @pl.when(side == 1)
    def _():
        piece(other_ref, own_ref, HALF)


def update_piece(own, other, mean):
    return pl.pallas_call(
        update_kernel,
        out_shape=jax.ShapeDtypeStruct((BLOCK, HALF), jnp.bfloat16),
        compiler_params=pltpu.CompilerParams(vmem_limit_bytes=32 * 1024 * 1024),
    )(own, other, mean)


def swap_cores(x):
    return lax.ppermute(x, "core", [(0, 1), (1, 0)])


def per_device(gradients):
    send = relayout(gradients[0])
    arrived = lax.all_to_all(send, ("x", "y", "z"), split_axis=0, concat_axis=0, tiled=True)
    blocks = arrived.reshape(PER_STRIP, BLOCK, BLOCK)
    (other,) = gram(send_kernel, (HALF + QUARTER,), blocks)
    stat_other = swap_cores(other)
    keep, mean_own = gram(keep_kernel, (HALF + QUARTER, BLOCK), blocks)
    mean_other = swap_cores(mean_own)
    own_root = inverse_root(keep, stat_other)
    other_root = swap_cores(own_root)
    piece = update_piece(own_root, other_root, mean_block(mean_own, mean_other))
    rows = lax.all_to_all(
        piece.reshape(STRIPS, 16, HALF), ("y", "z"), split_axis=0, concat_axis=0, tiled=True
    )
    return jnp.swapaxes(rows, 0, 1)[:, :, None, :]


def solution(mesh):
    fine = Mesh(mesh.devices.reshape(4, 2, 4, 8), ("x", "core", "y", "z"))
    return jax.shard_map(
        per_device,
        mesh=fine,
        in_specs=(P(("x", "core"), ("y", "z"), None),),
        out_specs=P(("y", "z"), None, ("x", "core"), None),
        check_vma=False,
    )
```

```python
import jax
import jax.numpy as jnp
from jax import lax
from jax.experimental import pallas as pl
from jax.experimental.pallas import tpu as pltpu
from jax.sharding import Mesh
from jax.sharding import PartitionSpec as P

ITERS = 6
GROUPS = 8
BLOCK = 512
PER_STRIP = 4
STRIPS = 32
HALF = 256
QUARTER = 128
CHUNKS = 8
CHUNK = 8192


def dot_nn(a, b):
    return lax.dot_general(a, b, (((1,), (0,)), ((), ())), preferred_element_type=jnp.float32)


def dot_nt(a, b):
    return lax.dot_general(a, b, (((1,), (1,)), ((), ())), preferred_element_type=jnp.float32)


def dot_tn(a, b):
    return lax.dot_general(a, b, (((0,), (0,)), ((), ())), preferred_element_type=jnp.float32)


def split_product(a, b):
    a_high, b_high = a.astype(jnp.bfloat16), b.astype(jnp.bfloat16)
    a_low = (a - a_high.astype(jnp.float32)).astype(jnp.bfloat16)
    b_low = (b - b_high.astype(jnp.float32)).astype(jnp.bfloat16)
    return dot_nn(
        jnp.concatenate([a_high, a_high, a_low], axis=1),
        jnp.concatenate([b_high, b_low, b_high], axis=0),
    )


def relayout_kernel(in_ref, out_ref, landed, sems):
    copies = []
    for chunk in range(CHUNKS):
        columns = pl.ds(chunk * CHUNK, CHUNK)
        copies.append(
            pltpu.make_async_copy(in_ref.at[:, columns], landed.at[:, columns], sems.at[chunk])
        )
        copies[-1].start()
    for chunk in range(CHUNKS):
        copies[chunk].wait()
        for index in range(chunk * CHUNK // BLOCK, (chunk + 1) * CHUNK // BLOCK):
            strip, k = divmod(index, PER_STRIP)
            out_ref[k * STRIPS + strip] = landed[:, index * BLOCK : (index + 1) * BLOCK]


def relayout(rows):
    return pl.pallas_call(
        relayout_kernel,
        in_specs=[pl.BlockSpec(memory_space=pl.ANY)],
        out_specs=pl.BlockSpec(memory_space=pltpu.VMEM),
        out_shape=jax.ShapeDtypeStruct((PER_STRIP * STRIPS, 16, BLOCK), jnp.bfloat16),
        scratch_shapes=[
            pltpu.VMEM((16, STRIPS * PER_STRIP * BLOCK), jnp.bfloat16),
            pltpu.SemaphoreType.DMA((CHUNKS,)),
        ],
        compiler_params=pltpu.CompilerParams(vmem_limit_bytes=50 * 1024 * 1024),
    )(rows)


def left_gram(in_ref, out_ref):
    wide = jnp.concatenate([in_ref[g] for g in range(PER_STRIP)], axis=1)
    low = wide[HALF:]
    store_gram(dot_nt(wide[:HALF], wide), dot_nt(low, low), out_ref)


def right_gram(in_ref, out_ref):
    tall = in_ref[...].reshape(PER_STRIP * BLOCK, BLOCK)
    low = tall[:, HALF:]
    store_gram(dot_tn(tall[:, :HALF], tall), dot_tn(low, low), out_ref)


def store_gram(top, corner, out_ref):
    out_ref[:HALF] = top
    out_ref[HALF:, :HALF] = corner[:QUARTER]
    out_ref[HALF:, HALF:] = corner[QUARTER:]


def send_kernel(in_ref, send_ref):
    side = lax.axis_index("core")

    @pl.when(side == 0)
    def _():
        right_gram(in_ref, send_ref)

    @pl.when(side == 1)
    def _():
        left_gram(in_ref, send_ref)


def keep_kernel(in_ref, keep_ref, mean_ref):
    side = lax.axis_index("core")

    @pl.when(side == 0)
    def _():
        left_gram(in_ref, keep_ref)

    @pl.when(side == 1)
    def _():
        right_gram(in_ref, keep_ref)

    total = in_ref[0].astype(jnp.float32)
    for group in range(1, PER_STRIP):
        total += in_ref[group].astype(jnp.float32)
    mean_ref[...] = total


def gram(kernel, rows, blocks):
    return pl.pallas_call(
        kernel,
        out_shape=[jax.ShapeDtypeStruct((n, BLOCK), jnp.float32) for n in rows],
        compiler_params=pltpu.CompilerParams(vmem_limit_bytes=32 * 1024 * 1024),
        cost_estimate=pl.CostEstimate(
            flops=4 * 2 * BLOCK**3, bytes_accessed=16 * BLOCK * BLOCK, transcendentals=0
        ),
    )(blocks)


def root_kernel(own_ref, other_ref, out_ref):
    row = lax.broadcasted_iota(jnp.int32, (QUARTER, QUARTER), 0)
    col = lax.broadcasted_iota(jnp.int32, (QUARTER, QUARTER), 1)
    diagonal = row == col
    tiles = [slice(start, start + QUARTER) for start in range(0, BLOCK, QUARTER)]
    packed = own_ref[...] + other_ref[...]
    low = jnp.concatenate([packed[HALF:, :HALF], packed[HALF:, HALF:]], axis=0)
    low = jnp.concatenate([packed[:HALF, HALF:].T, low], axis=1)
    stat = jnp.concatenate([packed[:HALF], low], axis=0)
    on_diagonal = sum(jnp.where(diagonal, stat[tile, tile], 0.0) for tile in tiles)
    trace = jnp.sum(on_diagonal, keepdims=True)
    growth = 1.25**4
    f = stat * (0.2 / trace)
    y = None
    for iteration in range(ITERS - 1):
        fb = f.astype(jnp.bfloat16)
        f_squared = dot_nn(fb, fb)
        g = 2.0 * f - f_squared
        gb = g.astype(jnp.bfloat16)
        h = 2.0 * g - dot_nn(gb, gb)
        hb = h.astype(jnp.bfloat16)
        if iteration + 2 < ITERS:
            y = f if y is None else y + f - dot_nn(y.astype(jnp.bfloat16), fb)
            hf = split_product(h, f) if iteration == 0 else dot_nn(hb, fb)
            f = growth * (f - hf)
        else:
            af = f - f_squared
            w = f + growth * (af - dot_nn(hb, af.astype(jnp.bfloat16)))
            y = y + w - dot_nn(y.astype(jnp.bfloat16), w.astype(jnp.bfloat16))
    scale = lax.rsqrt(jnp.sqrt(trace * (1.0 / (GROUPS * BLOCK)))) * 1.25**ITERS
    out_ref[...] = (-scale * y).astype(jnp.bfloat16)
    for tile in tiles:
        x = scale * (jnp.where(diagonal, 1.0, 0.0) - y[tile, tile])
        out_ref[tile, tile] = x.astype(jnp.bfloat16)


def inverse_root(own, other):
    return pl.pallas_call(
        root_kernel,
        out_shape=jax.ShapeDtypeStruct((BLOCK, BLOCK), jnp.bfloat16),
        compiler_params=pltpu.CompilerParams(vmem_limit_bytes=48 * 1024 * 1024),
        cost_estimate=pl.CostEstimate(
            flops=20 * 2 * BLOCK**3, bytes_accessed=10 * BLOCK * BLOCK, transcendentals=0
        ),
    )(own, other)


def mean_kernel(own_ref, other_ref, out_ref):
    out_ref[...] = ((own_ref[...] + other_ref[...]) * (1.0 / GROUPS)).astype(jnp.bfloat16)


def mean_block(own, other):
    return pl.pallas_call(
        mean_kernel,
        out_shape=jax.ShapeDtypeStruct((BLOCK, BLOCK), jnp.bfloat16),
        compiler_params=pltpu.CompilerParams(vmem_limit_bytes=16 * 1024 * 1024),
        cost_estimate=pl.CostEstimate(
            flops=2 * BLOCK * BLOCK, bytes_accessed=10 * BLOCK * BLOCK, transcendentals=0
        ),
    )(own, other)


def update_kernel(own_ref, other_ref, mean_ref, out_ref):
    side = lax.axis_index("core")

    def piece(left_ref, right_ref, start):
        right = right_ref[:, start : start + HALF]
        inner = dot_nn(mean_ref[...], right).astype(jnp.bfloat16)
        out_ref[...] = dot_nn(left_ref[...], inner).astype(jnp.bfloat16)

    @pl.when(side == 0)
    def _():
        piece(own_ref, other_ref, 0)

    @pl.when(side == 1)
    def _():
        piece(other_ref, own_ref, HALF)


def update_piece(own, other, mean):
    return pl.pallas_call(
        update_kernel,
        out_shape=jax.ShapeDtypeStruct((BLOCK, HALF), jnp.bfloat16),
        compiler_params=pltpu.CompilerParams(vmem_limit_bytes=32 * 1024 * 1024),
    )(own, other, mean)


def swap_cores(x):
    return lax.ppermute(x, "core", [(0, 1), (1, 0)])


def per_device(gradients):
    send = relayout(gradients[0])
    arrived = lax.all_to_all(send, ("x", "y", "z"), split_axis=0, concat_axis=0, tiled=True)
    blocks = arrived.reshape(PER_STRIP, BLOCK, BLOCK)
    (other,) = gram(send_kernel, (HALF + QUARTER,), blocks)
    stat_other = swap_cores(other)
    keep, mean_own = gram(keep_kernel, (HALF + QUARTER, BLOCK), blocks)
    mean_other = swap_cores(mean_own)
    own_root = inverse_root(keep, stat_other)
    other_root = swap_cores(own_root)
    piece = update_piece(own_root, other_root, mean_block(mean_own, mean_other))
    rows = lax.all_to_all(
        piece.reshape(STRIPS, 16, HALF), ("y", "z"), split_axis=0, concat_axis=0, tiled=True
    )
    return jnp.swapaxes(rows, 0, 1)[:, :, None, :]


def solution(mesh):
    fine = Mesh(mesh.devices.reshape(4, 2, 4, 8), ("x", "core", "y", "z"))
    return jax.shard_map(
        per_device,
        mesh=fine,
        in_specs=(P(("x", "core"), ("y", "z"), None),),
        out_specs=P(("y", "z"), None, ("x", "core"), None),
        check_vma=False,
    )
```

```python
import jax
import jax.numpy as jnp
from jax import lax
from jax.experimental import pallas as pl
from jax.experimental.pallas import tpu as pltpu
from jax.sharding import Mesh
from jax.sharding import PartitionSpec as P

ITERS = 6
GROUPS = 8
BLOCK = 512
PER_STRIP = 4
STRIPS = 32
HALF = 256
QUARTER = 128
CHUNKS = 8
CHUNK = 8192


def dot_nn(a, b):
    return lax.dot_general(a, b, (((1,), (0,)), ((), ())), preferred_element_type=jnp.float32)


def dot_nt(a, b):
    return lax.dot_general(a, b, (((1,), (1,)), ((), ())), preferred_element_type=jnp.float32)


def dot_tn(a, b):
    return lax.dot_general(a, b, (((0,), (0,)), ((), ())), preferred_element_type=jnp.float32)


def split_product(a, b):
    a_high, b_high = a.astype(jnp.bfloat16), b.astype(jnp.bfloat16)
    a_low = (a - a_high.astype(jnp.float32)).astype(jnp.bfloat16)
    b_low = (b - b_high.astype(jnp.float32)).astype(jnp.bfloat16)
    return dot_nn(
        jnp.concatenate([a_high, a_high, a_low], axis=1),
        jnp.concatenate([b_high, b_low, b_high], axis=0),
    )


def relayout_kernel(in_ref, out_ref, landed, sems):
    copies = []
    for chunk in range(CHUNKS):
        columns = pl.ds(chunk * CHUNK, CHUNK)
        copies.append(
            pltpu.make_async_copy(in_ref.at[:, columns], landed.at[:, columns], sems.at[chunk])
        )
        copies[-1].start()
    for chunk in range(CHUNKS):
        copies[chunk].wait()
        for index in range(chunk * CHUNK // BLOCK, (chunk + 1) * CHUNK // BLOCK):
            out_ref[index] = landed[:, index * BLOCK : (index + 1) * BLOCK]


def relayout(rows):
    return pl.pallas_call(
        relayout_kernel,
        in_specs=[pl.BlockSpec(memory_space=pl.ANY)],
        out_specs=pl.BlockSpec(memory_space=pltpu.VMEM),
        out_shape=jax.ShapeDtypeStruct((PER_STRIP * STRIPS, 16, BLOCK), jnp.bfloat16),
        scratch_shapes=[
            pltpu.VMEM((16, STRIPS * PER_STRIP * BLOCK), jnp.bfloat16),
            pltpu.SemaphoreType.DMA((CHUNKS,)),
        ],
        compiler_params=pltpu.CompilerParams(vmem_limit_bytes=50 * 1024 * 1024),
    )(rows)


def group_block(in_ref, group):
    return in_ref[:, group].reshape(BLOCK, BLOCK)


def left_gram(in_ref, out_ref):
    wide = jnp.concatenate([group_block(in_ref, g) for g in range(PER_STRIP)], axis=1)
    low = wide[HALF:]
    store_gram(dot_nt(wide[:HALF], wide), dot_nt(low, low), out_ref)


def right_gram(in_ref, out_ref):
    tall = in_ref[...].reshape(PER_STRIP * BLOCK, BLOCK)
    low = tall[:, HALF:]
    store_gram(dot_tn(tall[:, :HALF], tall), dot_tn(low, low), out_ref)


def store_gram(top, corner, out_ref):
    out_ref[:HALF] = top
    out_ref[HALF:, :HALF] = corner[:QUARTER]
    out_ref[HALF:, HALF:] = corner[QUARTER:]


def send_kernel(in_ref, send_ref):
    side = lax.axis_index("core")

    @pl.when(side == 0)
    def _():
        right_gram(in_ref, send_ref)

    @pl.when(side == 1)
    def _():
        left_gram(in_ref, send_ref)


def keep_kernel(in_ref, keep_ref, mean_ref):
    side = lax.axis_index("core")

    @pl.when(side == 0)
    def _():
        left_gram(in_ref, keep_ref)

    @pl.when(side == 1)
    def _():
        right_gram(in_ref, keep_ref)

    total = group_block(in_ref, 0).astype(jnp.float32)
    for group in range(1, PER_STRIP):
        total += group_block(in_ref, group).astype(jnp.float32)
    mean_ref[...] = total


def gram(kernel, rows, blocks):
    return pl.pallas_call(
        kernel,
        out_shape=[jax.ShapeDtypeStruct((n, BLOCK), jnp.float32) for n in rows],
        compiler_params=pltpu.CompilerParams(vmem_limit_bytes=32 * 1024 * 1024),
        cost_estimate=pl.CostEstimate(
            flops=4 * 2 * BLOCK**3, bytes_accessed=16 * BLOCK * BLOCK, transcendentals=0
        ),
    )(blocks)


def root_kernel(own_ref, other_ref, out_ref):
    row = lax.broadcasted_iota(jnp.int32, (QUARTER, QUARTER), 0)
    col = lax.broadcasted_iota(jnp.int32, (QUARTER, QUARTER), 1)
    diagonal = row == col
    tiles = [slice(start, start + QUARTER) for start in range(0, BLOCK, QUARTER)]
    packed = own_ref[...] + other_ref[...]
    low = jnp.concatenate([packed[HALF:, :HALF], packed[HALF:, HALF:]], axis=0)
    low = jnp.concatenate([packed[:HALF, HALF:].T, low], axis=1)
    stat = jnp.concatenate([packed[:HALF], low], axis=0)
    on_diagonal = sum(jnp.where(diagonal, stat[tile, tile], 0.0) for tile in tiles)
    trace = jnp.sum(on_diagonal, keepdims=True)
    growth = 1.25**4
    f = stat * (0.2 / trace)
    y = None
    for iteration in range(ITERS - 1):
        fb = f.astype(jnp.bfloat16)
        f_squared = dot_nn(fb, fb)
        g = 2.0 * f - f_squared
        gb = g.astype(jnp.bfloat16)
        h = 2.0 * g - dot_nn(gb, gb)
        hb = h.astype(jnp.bfloat16)
        if iteration + 2 < ITERS:
            y = f if y is None else y + f - dot_nn(y.astype(jnp.bfloat16), fb)
            hf = split_product(h, f) if iteration == 0 else dot_nn(hb, fb)
            f = growth * (f - hf)
        else:
            af = f - f_squared
            w = f + growth * (af - dot_nn(hb, af.astype(jnp.bfloat16)))
            y = y + w - dot_nn(y.astype(jnp.bfloat16), w.astype(jnp.bfloat16))
    scale = lax.rsqrt(jnp.sqrt(trace * (1.0 / (GROUPS * BLOCK)))) * 1.25**ITERS
    out_ref[...] = (-scale * y).astype(jnp.bfloat16)
    for tile in tiles:
        x = scale * (jnp.where(diagonal, 1.0, 0.0) - y[tile, tile])
        out_ref[tile, tile] = x.astype(jnp.bfloat16)


def inverse_root(own, other):
    return pl.pallas_call(
        root_kernel,
        out_shape=jax.ShapeDtypeStruct((BLOCK, BLOCK), jnp.bfloat16),
        compiler_params=pltpu.CompilerParams(vmem_limit_bytes=48 * 1024 * 1024),
        cost_estimate=pl.CostEstimate(
            flops=20 * 2 * BLOCK**3, bytes_accessed=10 * BLOCK * BLOCK, transcendentals=0
        ),
    )(own, other)


def mean_kernel(own_ref, other_ref, out_ref):
    out_ref[...] = ((own_ref[...] + other_ref[...]) * (1.0 / GROUPS)).astype(jnp.bfloat16)


def mean_block(own, other):
    return pl.pallas_call(
        mean_kernel,
        out_shape=jax.ShapeDtypeStruct((BLOCK, BLOCK), jnp.bfloat16),
        compiler_params=pltpu.CompilerParams(vmem_limit_bytes=16 * 1024 * 1024),
        cost_estimate=pl.CostEstimate(
            flops=2 * BLOCK * BLOCK, bytes_accessed=10 * BLOCK * BLOCK, transcendentals=0
        ),
    )(own, other)


def update_kernel(own_ref, other_ref, mean_ref, out_ref):
    side = lax.axis_index("core")

    def piece(left_ref, right_ref, start):
        right = right_ref[:, start : start + HALF]
        inner = dot_nn(mean_ref[...], right).astype(jnp.bfloat16)
        out_ref[...] = dot_nn(left_ref[...], inner).astype(jnp.bfloat16)

    @pl.when(side == 0)
    def _():
        piece(own_ref, other_ref, 0)

    @pl.when(side == 1)
    def _():
        piece(other_ref, own_ref, HALF)


def update_piece(own, other, mean):
    return pl.pallas_call(
        update_kernel,
        out_shape=jax.ShapeDtypeStruct((BLOCK, HALF), jnp.bfloat16),
        compiler_params=pltpu.CompilerParams(vmem_limit_bytes=32 * 1024 * 1024),
    )(own, other, mean)


def swap_cores(x):
    return lax.ppermute(x, "core", [(0, 1), (1, 0)])


def per_device(gradients):
    send = relayout(gradients[0])
    arrived = lax.all_to_all(send, ("y", "z", "x"), split_axis=0, concat_axis=0, tiled=True)
    blocks = arrived.reshape(STRIPS, PER_STRIP, 16, BLOCK)
    (other,) = gram(send_kernel, (HALF + QUARTER,), blocks)
    stat_other = swap_cores(other)
    keep, mean_own = gram(keep_kernel, (HALF + QUARTER, BLOCK), blocks)
    mean_other = swap_cores(mean_own)
    own_root = inverse_root(keep, stat_other)
    other_root = swap_cores(own_root)
    piece = update_piece(own_root, other_root, mean_block(mean_own, mean_other))
    rows = lax.all_to_all(
        piece.reshape(STRIPS, 16, HALF), ("y", "z"), split_axis=0, concat_axis=0, tiled=True
    )
    return jnp.swapaxes(rows, 0, 1)[:, :, None, :]


def solution(mesh):
    fine = Mesh(mesh.devices.reshape(4, 2, 4, 8), ("x", "core", "y", "z"))
    return jax.shard_map(
        per_device,
        mesh=fine,
        in_specs=(P(("x", "core"), ("y", "z"), None),),
        out_specs=P(("y", "z"), None, ("x", "core"), None),
        check_vma=False,
    )
```

```python
import jax
import jax.numpy as jnp
from jax import lax
from jax.experimental import pallas as pl
from jax.experimental.pallas import tpu as pltpu
from jax.sharding import Mesh
from jax.sharding import PartitionSpec as P

ITERS = 6
GROUPS = 8
BLOCK = 512
PER_STRIP = 4
STRIPS = 32
HALF = 256
QUARTER = 128
DEPTH = 8
CHUNKS = 8
CHUNK = 8192


def dot_nn(a, b):
    return lax.dot_general(a, b, (((1,), (0,)), ((), ())), preferred_element_type=jnp.float32)


def dot_nt(a, b):
    return lax.dot_general(a, b, (((1,), (1,)), ((), ())), preferred_element_type=jnp.float32)


def dot_tn(a, b):
    return lax.dot_general(a, b, (((0,), (0,)), ((), ())), preferred_element_type=jnp.float32)


def split_product(a, b):
    a_high, b_high = a.astype(jnp.bfloat16), b.astype(jnp.bfloat16)
    a_low = (a - a_high.astype(jnp.float32)).astype(jnp.bfloat16)
    b_low = (b - b_high.astype(jnp.float32)).astype(jnp.bfloat16)
    return dot_nn(
        jnp.concatenate([a_high, a_high, a_low], axis=1),
        jnp.concatenate([b_high, b_low, b_high], axis=0),
    )


def relayout_kernel(in_ref, out_ref, landed, sems):
    copies = []
    for chunk in range(CHUNKS):
        columns = pl.ds(chunk * CHUNK, CHUNK)
        copies.append(
            pltpu.make_async_copy(in_ref.at[:, columns], landed.at[:, columns], sems.at[chunk])
        )
        copies[-1].start()
    for chunk in range(CHUNKS):
        copies[chunk].wait()
        for index in range(chunk * CHUNK // BLOCK, (chunk + 1) * CHUNK // BLOCK):
            out_ref[index] = landed[:, index * BLOCK : (index + 1) * BLOCK]


def relayout(rows):
    return pl.pallas_call(
        relayout_kernel,
        in_specs=[pl.BlockSpec(memory_space=pl.ANY)],
        out_specs=pl.BlockSpec(memory_space=pltpu.VMEM),
        out_shape=jax.ShapeDtypeStruct((PER_STRIP * STRIPS, 16, BLOCK), jnp.bfloat16),
        scratch_shapes=[
            pltpu.VMEM((16, STRIPS * PER_STRIP * BLOCK), jnp.bfloat16),
            pltpu.SemaphoreType.DMA((CHUNKS,)),
        ],
        compiler_params=pltpu.CompilerParams(vmem_limit_bytes=50 * 1024 * 1024),
    )(rows)


def group_block(in_ref, group):
    return in_ref[:, group].reshape(BLOCK, BLOCK)


def left_gram(in_ref, out_ref):
    wide = jnp.concatenate([group_block(in_ref, g) for g in range(PER_STRIP)], axis=1)
    low = wide[HALF:]
    store_gram(dot_nt(wide[:HALF], wide), dot_nt(low, low), out_ref)


def right_gram(in_ref, out_ref):
    tall = in_ref[...].reshape(PER_STRIP * BLOCK, BLOCK)
    low = tall[:, HALF:]
    store_gram(dot_tn(tall[:, :HALF], tall), dot_tn(low, low), out_ref)


def store_gram(top, corner, out_ref):
    out_ref[:HALF] = top
    out_ref[HALF:, :HALF] = corner[:QUARTER]
    out_ref[HALF:, HALF:] = corner[QUARTER:]


def send_kernel(in_ref, send_ref):
    side = lax.axis_index("core")

    @pl.when(side == 0)
    def _():
        right_gram(in_ref, send_ref)

    @pl.when(side == 1)
    def _():
        left_gram(in_ref, send_ref)


def keep_kernel(in_ref, keep_ref, mean_ref):
    side = lax.axis_index("core")

    @pl.when(side == 0)
    def _():
        left_gram(in_ref, keep_ref)

    @pl.when(side == 1)
    def _():
        right_gram(in_ref, keep_ref)

    total = group_block(in_ref, 0).astype(jnp.float32)
    for group in range(1, PER_STRIP):
        total += group_block(in_ref, group).astype(jnp.float32)
    mean_ref[...] = total


def gram(kernel, rows, blocks):
    return pl.pallas_call(
        kernel,
        out_shape=[jax.ShapeDtypeStruct((n, BLOCK), jnp.float32) for n in rows],
        compiler_params=pltpu.CompilerParams(vmem_limit_bytes=32 * 1024 * 1024),
        cost_estimate=pl.CostEstimate(
            flops=4 * 2 * BLOCK**3, bytes_accessed=16 * BLOCK * BLOCK, transcendentals=0
        ),
    )(blocks)


def root_kernel(own_ref, other_ref, out_ref):
    row = lax.broadcasted_iota(jnp.int32, (QUARTER, QUARTER), 0)
    col = lax.broadcasted_iota(jnp.int32, (QUARTER, QUARTER), 1)
    diagonal = row == col
    tiles = [slice(start, start + QUARTER) for start in range(0, BLOCK, QUARTER)]
    packed = own_ref[...] + other_ref[...]
    low = jnp.concatenate([packed[HALF:, :HALF], packed[HALF:, HALF:]], axis=0)
    low = jnp.concatenate([packed[:HALF, HALF:].T, low], axis=1)
    stat = jnp.concatenate([packed[:HALF], low], axis=0)
    on_diagonal = sum(jnp.where(diagonal, stat[tile, tile], 0.0) for tile in tiles)
    trace = jnp.sum(on_diagonal, keepdims=True)
    growth = 1.25**4
    f = stat * (0.2 / trace)
    y = None
    for iteration in range(ITERS - 1):
        fb = f.astype(jnp.bfloat16)
        f_squared = dot_nn(fb, fb)
        g = 2.0 * f - f_squared
        gb = g.astype(jnp.bfloat16)
        h = 2.0 * g - dot_nn(gb, gb)
        hb = h.astype(jnp.bfloat16)
        if iteration + 2 < ITERS:
            y = f if y is None else y + f - dot_nn(y.astype(jnp.bfloat16), fb)
            hf = split_product(h, f) if iteration == 0 else dot_nn(hb, fb)
            f = growth * (f - hf)
        else:
            af = f - f_squared
            w = f + growth * (af - dot_nn(hb, af.astype(jnp.bfloat16)))
            y = y + w - dot_nn(y.astype(jnp.bfloat16), w.astype(jnp.bfloat16))
    scale = lax.rsqrt(jnp.sqrt(trace * (1.0 / (GROUPS * BLOCK)))) * 1.25**ITERS
    out_ref[...] = (-scale * y).astype(jnp.bfloat16)
    for tile in tiles:
        x = scale * (jnp.where(diagonal, 1.0, 0.0) - y[tile, tile])
        out_ref[tile, tile] = x.astype(jnp.bfloat16)


def inverse_root(own, other):
    return pl.pallas_call(
        root_kernel,
        out_shape=jax.ShapeDtypeStruct((BLOCK, BLOCK), jnp.bfloat16),
        compiler_params=pltpu.CompilerParams(vmem_limit_bytes=48 * 1024 * 1024),
        cost_estimate=pl.CostEstimate(
            flops=20 * 2 * BLOCK**3, bytes_accessed=10 * BLOCK * BLOCK, transcendentals=0
        ),
    )(own, other)


def mean_kernel(own_ref, other_ref, out_ref):
    out_ref[...] = ((own_ref[...] + other_ref[...]) * (1.0 / GROUPS)).astype(jnp.bfloat16)


def mean_block(own, other):
    return pl.pallas_call(
        mean_kernel,
        out_shape=jax.ShapeDtypeStruct((BLOCK, BLOCK), jnp.bfloat16),
        compiler_params=pltpu.CompilerParams(vmem_limit_bytes=16 * 1024 * 1024),
        cost_estimate=pl.CostEstimate(
            flops=2 * BLOCK * BLOCK, bytes_accessed=10 * BLOCK * BLOCK, transcendentals=0
        ),
    )(own, other)


def update_kernel(own_ref, other_ref, mean_ref, out_ref):
    side = lax.axis_index("core")

    def piece(left_ref, right_ref, start):
        right = right_ref[:, start : start + HALF]
        inner = dot_nn(mean_ref[...], right).astype(jnp.bfloat16)
        update = dot_nn(left_ref[...], inner).astype(jnp.bfloat16)
        update = update.reshape(STRIPS, 16, HALF)
        for y in range(STRIPS // DEPTH):
            for z in range(DEPTH):
                out_ref[z, y] = update[y * DEPTH + z]

    @pl.when(side == 0)
    def _():
        piece(own_ref, other_ref, 0)

    @pl.when(side == 1)
    def _():
        piece(other_ref, own_ref, HALF)


def update_piece(own, other, mean):
    return pl.pallas_call(
        update_kernel,
        out_shape=jax.ShapeDtypeStruct((DEPTH, STRIPS // DEPTH, 16, HALF), jnp.bfloat16),
        compiler_params=pltpu.CompilerParams(vmem_limit_bytes=32 * 1024 * 1024),
    )(own, other, mean)


def swap_cores(x):
    return lax.ppermute(x, "core", [(0, 1), (1, 0)])


def per_device(gradients):
    send = relayout(gradients[0])
    arrived = lax.all_to_all(send, ("y", "z", "x"), split_axis=0, concat_axis=0, tiled=True)
    blocks = arrived.reshape(STRIPS, PER_STRIP, 16, BLOCK)
    (other,) = gram(send_kernel, (HALF + QUARTER,), blocks)
    stat_other = swap_cores(other)
    keep, mean_own = gram(keep_kernel, (HALF + QUARTER, BLOCK), blocks)
    mean_other = swap_cores(mean_own)
    own_root = inverse_root(keep, stat_other)
    other_root = swap_cores(own_root)
    piece = update_piece(own_root, other_root, mean_block(mean_own, mean_other))
    rows = lax.all_to_all(
        piece.reshape(STRIPS, 16, HALF), ("z", "y"), split_axis=0, concat_axis=0, tiled=True
    )
    rows = rows.reshape(DEPTH, STRIPS // DEPTH, 16, HALF).transpose(2, 1, 0, 3)
    return rows.reshape(16, STRIPS, 1, HALF)


def solution(mesh):
    fine = Mesh(mesh.devices.reshape(4, 2, 4, 8), ("x", "core", "y", "z"))
    return jax.shard_map(
        per_device,
        mesh=fine,
        in_specs=(P(("x", "core"), ("y", "z"), None),),
        out_specs=P(("y", "z"), None, ("x", "core"), None),
        check_vma=False,
    )
```

```python
import jax
import jax.numpy as jnp
from jax import lax
from jax.experimental import pallas as pl
from jax.experimental.pallas import tpu as pltpu
from jax.sharding import Mesh
from jax.sharding import PartitionSpec as P

ITERS = 6
GROUPS = 8
BLOCK = 512
PER_STRIP = 4
STRIPS = 32
HALF = 256
QUARTER = 128
CHUNKS = 8
CHUNK = 8192


def dot_nn(a, b):
    return lax.dot_general(a, b, (((1,), (0,)), ((), ())), preferred_element_type=jnp.float32)


def dot_nt(a, b):
    return lax.dot_general(a, b, (((1,), (1,)), ((), ())), preferred_element_type=jnp.float32)


def dot_tn(a, b):
    return lax.dot_general(a, b, (((0,), (0,)), ((), ())), preferred_element_type=jnp.float32)


def split_product(a, b):
    a_high, b_high = a.astype(jnp.bfloat16), b.astype(jnp.bfloat16)
    a_low = (a - a_high.astype(jnp.float32)).astype(jnp.bfloat16)
    b_low = (b - b_high.astype(jnp.float32)).astype(jnp.bfloat16)
    return dot_nn(
        jnp.concatenate([a_high, a_high, a_low], axis=1),
        jnp.concatenate([b_high, b_low, b_high], axis=0),
    )


def relayout_kernel(in_ref, out_ref, landed, sems):
    copies = []
    for chunk in range(CHUNKS):
        columns = pl.ds(chunk * CHUNK, CHUNK)
        copies.append(
            pltpu.make_async_copy(in_ref.at[:, columns], landed.at[:, columns], sems.at[chunk])
        )
        copies[-1].start()
    for chunk in range(CHUNKS):
        copies[chunk].wait()
        for index in range(chunk * CHUNK // BLOCK, (chunk + 1) * CHUNK // BLOCK):
            out_ref[index] = landed[:, index * BLOCK : (index + 1) * BLOCK]


def relayout(rows):
    return pl.pallas_call(
        relayout_kernel,
        in_specs=[pl.BlockSpec(memory_space=pl.ANY)],
        out_specs=pl.BlockSpec(memory_space=pltpu.VMEM),
        out_shape=jax.ShapeDtypeStruct((PER_STRIP * STRIPS, 16, BLOCK), jnp.bfloat16),
        scratch_shapes=[
            pltpu.VMEM((16, STRIPS * PER_STRIP * BLOCK), jnp.bfloat16),
            pltpu.SemaphoreType.DMA((CHUNKS,)),
        ],
        compiler_params=pltpu.CompilerParams(vmem_limit_bytes=50 * 1024 * 1024),
    )(rows)


def group_block(in_ref, group):
    return in_ref[:, group].reshape(BLOCK, BLOCK)


def left_gram(in_ref, out_ref):
    wide = jnp.concatenate([group_block(in_ref, g) for g in range(PER_STRIP)], axis=1)
    low = wide[HALF:]
    store_gram(dot_nt(wide[:HALF], wide), dot_nt(low, low), out_ref)


def right_gram(in_ref, out_ref):
    tall = in_ref[...].reshape(PER_STRIP * BLOCK, BLOCK)
    low = tall[:, HALF:]
    store_gram(dot_tn(tall[:, :HALF], tall), dot_tn(low, low), out_ref)


def store_gram(top, corner, out_ref):
    out_ref[:HALF] = top
    out_ref[HALF:, :HALF] = corner[:QUARTER]
    out_ref[HALF:, HALF:] = corner[QUARTER:]


def send_kernel(in_ref, send_ref):
    side = lax.axis_index("core")

    @pl.when(side == 0)
    def _():
        right_gram(in_ref, send_ref)

    @pl.when(side == 1)
    def _():
        left_gram(in_ref, send_ref)


def keep_kernel(in_ref, keep_ref, mean_ref):
    side = lax.axis_index("core")

    @pl.when(side == 0)
    def _():
        left_gram(in_ref, keep_ref)

    @pl.when(side == 1)
    def _():
        right_gram(in_ref, keep_ref)

    total = group_block(in_ref, 0).astype(jnp.float32)
    for group in range(1, PER_STRIP):
        total += group_block(in_ref, group).astype(jnp.float32)
    mean_ref[...] = total


def gram(kernel, rows, blocks):
    return pl.pallas_call(
        kernel,
        out_shape=[jax.ShapeDtypeStruct((n, BLOCK), jnp.float32) for n in rows],
        compiler_params=pltpu.CompilerParams(vmem_limit_bytes=32 * 1024 * 1024),
        cost_estimate=pl.CostEstimate(
            flops=4 * 2 * BLOCK**3, bytes_accessed=16 * BLOCK * BLOCK, transcendentals=0
        ),
    )(blocks)


def halves(matrix):
    return [matrix[:HALF], matrix[HALF:]]


def as_bf16(parts):
    return jnp.concatenate([part.astype(jnp.bfloat16) for part in parts])


def root_kernel(own_ref, other_ref, out_ref):
    row = lax.broadcasted_iota(jnp.int32, (QUARTER, QUARTER), 0)
    col = lax.broadcasted_iota(jnp.int32, (QUARTER, QUARTER), 1)
    diagonal = row == col
    tiles = [slice(start, start + QUARTER) for start in range(0, BLOCK, QUARTER)]
    packed = own_ref[...] + other_ref[...]
    low = jnp.concatenate([packed[HALF:, :HALF], packed[HALF:, HALF:]], axis=0)
    low = jnp.concatenate([packed[:HALF, HALF:].T, low], axis=1)
    stat = jnp.concatenate([packed[:HALF], low], axis=0)
    on_diagonal = sum(jnp.where(diagonal, stat[tile, tile], 0.0) for tile in tiles)
    trace = jnp.sum(on_diagonal, keepdims=True)
    growth = 1.25**4
    f = halves(stat * (0.2 / trace))
    y = None
    for iteration in range(ITERS - 1):
        fb = as_bf16(f)
        f_squared = [dot_nn(part.astype(jnp.bfloat16), fb) for part in f]
        g = [2.0 * part - square for part, square in zip(f, f_squared)]
        gb = as_bf16(g)
        h = [2.0 * part - dot_nn(part.astype(jnp.bfloat16), gb) for part in g]
        if iteration + 2 < ITERS:
            if iteration == 0:
                hf = halves(split_product(jnp.concatenate(h), jnp.concatenate(f)))
            else:
                hf = [dot_nn(part.astype(jnp.bfloat16), fb) for part in h]
            if y is None:
                y = f
            else:
                y = [p + q - dot_nn(p.astype(jnp.bfloat16), fb) for p, q in zip(y, f)]
            f = [growth * (part - product) for part, product in zip(f, hf)]
        else:
            af = [part - square for part, square in zip(f, f_squared)]
            afb = as_bf16(af)
            haf = [dot_nn(part.astype(jnp.bfloat16), afb) for part in h]
            w = [p + growth * (q - product) for p, q, product in zip(f, af, haf)]
            wb = as_bf16(w)
            y = [p + q - dot_nn(p.astype(jnp.bfloat16), wb) for p, q in zip(y, w)]
    y = jnp.concatenate(y)
    scale = lax.rsqrt(jnp.sqrt(trace * (1.0 / (GROUPS * BLOCK)))) * 1.25**ITERS
    out_ref[...] = (-scale * y).astype(jnp.bfloat16)
    for tile in tiles:
        x = scale * (jnp.where(diagonal, 1.0, 0.0) - y[tile, tile])
        out_ref[tile, tile] = x.astype(jnp.bfloat16)


def inverse_root(own, other):
    return pl.pallas_call(
        root_kernel,
        out_shape=jax.ShapeDtypeStruct((BLOCK, BLOCK), jnp.bfloat16),
        compiler_params=pltpu.CompilerParams(vmem_limit_bytes=48 * 1024 * 1024),
        cost_estimate=pl.CostEstimate(
            flops=20 * 2 * BLOCK**3, bytes_accessed=10 * BLOCK * BLOCK, transcendentals=0
        ),
    )(own, other)


def mean_kernel(own_ref, other_ref, out_ref):
    out_ref[...] = ((own_ref[...] + other_ref[...]) * (1.0 / GROUPS)).astype(jnp.bfloat16)


def mean_block(own, other):
    return pl.pallas_call(
        mean_kernel,
        out_shape=jax.ShapeDtypeStruct((BLOCK, BLOCK), jnp.bfloat16),
        compiler_params=pltpu.CompilerParams(vmem_limit_bytes=16 * 1024 * 1024),
        cost_estimate=pl.CostEstimate(
            flops=2 * BLOCK * BLOCK, bytes_accessed=10 * BLOCK * BLOCK, transcendentals=0
        ),
    )(own, other)


def update_kernel(own_ref, other_ref, mean_ref, out_ref):
    side = lax.axis_index("core")

    def piece(left_ref, right_ref, start):
        right = right_ref[:, start : start + HALF]
        inner = dot_nn(mean_ref[...], right).astype(jnp.bfloat16)
        out_ref[...] = dot_nn(left_ref[...], inner).astype(jnp.bfloat16)

    @pl.when(side == 0)
    def _():
        piece(own_ref, other_ref, 0)

    @pl.when(side == 1)
    def _():
        piece(other_ref, own_ref, HALF)


def update_piece(own, other, mean):
    return pl.pallas_call(
        update_kernel,
        out_shape=jax.ShapeDtypeStruct((BLOCK, HALF), jnp.bfloat16),
        compiler_params=pltpu.CompilerParams(vmem_limit_bytes=32 * 1024 * 1024),
    )(own, other, mean)


def swap_cores(x):
    return lax.ppermute(x, "core", [(0, 1), (1, 0)])


def per_device(gradients):
    send = relayout(gradients[0])
    arrived = lax.all_to_all(send, ("y", "z", "x"), split_axis=0, concat_axis=0, tiled=True)
    blocks = arrived.reshape(STRIPS, PER_STRIP, 16, BLOCK)
    (other,) = gram(send_kernel, (HALF + QUARTER,), blocks)
    stat_other = swap_cores(other)
    keep, mean_own = gram(keep_kernel, (HALF + QUARTER, BLOCK), blocks)
    mean_other = swap_cores(mean_own)
    own_root = inverse_root(keep, stat_other)
    other_root = swap_cores(own_root)
    piece = update_piece(own_root, other_root, mean_block(mean_own, mean_other))
    rows = lax.all_to_all(
        piece.reshape(STRIPS, 16, HALF), ("y", "z"), split_axis=0, concat_axis=0, tiled=True
    )
    return jnp.swapaxes(rows, 0, 1)[:, :, None, :]


def solution(mesh):
    fine = Mesh(mesh.devices.reshape(4, 2, 4, 8), ("x", "core", "y", "z"))
    return jax.shard_map(
        per_device,
        mesh=fine,
        in_specs=(P(("x", "core"), ("y", "z"), None),),
        out_specs=P(("y", "z"), None, ("x", "core"), None),
        check_vma=False,
    )
```

```python
import jax
import jax.numpy as jnp
from jax import lax
from jax.experimental import pallas as pl
from jax.experimental.pallas import tpu as pltpu
from jax.sharding import Mesh
from jax.sharding import PartitionSpec as P

ITERS = 6
GROUPS = 8
BLOCK = 512
PER_STRIP = 4
STRIPS = 32
HALF = 256
QUARTER = 128
CHUNKS = 8
CHUNK = 8192


def dot_nn(a, b):
    return lax.dot_general(a, b, (((1,), (0,)), ((), ())), preferred_element_type=jnp.float32)


def dot_nt(a, b):
    return lax.dot_general(a, b, (((1,), (1,)), ((), ())), preferred_element_type=jnp.float32)


def dot_tn(a, b):
    return lax.dot_general(a, b, (((0,), (0,)), ((), ())), preferred_element_type=jnp.float32)


def split_product(a, b):
    a_high, b_high = a.astype(jnp.bfloat16), b.astype(jnp.bfloat16)
    a_low = (a - a_high.astype(jnp.float32)).astype(jnp.bfloat16)
    b_low = (b - b_high.astype(jnp.float32)).astype(jnp.bfloat16)
    return dot_nn(
        jnp.concatenate([a_high, a_high, a_low], axis=1),
        jnp.concatenate([b_high, b_low, b_high], axis=0),
    )


def relayout_kernel(in_ref, out_ref, landed, sems):
    copies = []
    for chunk in range(CHUNKS):
        columns = pl.ds(chunk * CHUNK, CHUNK)
        copies.append(
            pltpu.make_async_copy(in_ref.at[:, columns], landed.at[:, columns], sems.at[chunk])
        )
        copies[-1].start()
    for chunk in range(CHUNKS):
        copies[chunk].wait()
        for index in range(chunk * CHUNK // BLOCK, (chunk + 1) * CHUNK // BLOCK):
            out_ref[index] = landed[:, index * BLOCK : (index + 1) * BLOCK]


def relayout(rows):
    return pl.pallas_call(
        relayout_kernel,
        in_specs=[pl.BlockSpec(memory_space=pl.ANY)],
        out_specs=pl.BlockSpec(memory_space=pltpu.VMEM),
        out_shape=jax.ShapeDtypeStruct((PER_STRIP * STRIPS, 16, BLOCK), jnp.bfloat16),
        scratch_shapes=[
            pltpu.VMEM((16, STRIPS * PER_STRIP * BLOCK), jnp.bfloat16),
            pltpu.SemaphoreType.DMA((CHUNKS,)),
        ],
        compiler_params=pltpu.CompilerParams(vmem_limit_bytes=50 * 1024 * 1024),
    )(rows)


def group_block(in_ref, group):
    return in_ref[:, group].reshape(BLOCK, BLOCK)


def left_gram(in_ref, out_ref):
    wide = jnp.concatenate([group_block(in_ref, g) for g in range(PER_STRIP)], axis=1)
    low = wide[HALF:]
    store_gram(dot_nt(wide[:HALF], wide), dot_nt(low, low), out_ref)


def right_gram(in_ref, out_ref):
    tall = in_ref[...].reshape(PER_STRIP * BLOCK, BLOCK)
    low = tall[:, HALF:]
    store_gram(dot_tn(tall[:, :HALF], tall), dot_tn(low, low), out_ref)


def store_gram(top, corner, out_ref):
    out_ref[:HALF] = top
    out_ref[HALF:, :HALF] = corner[:QUARTER]
    out_ref[HALF:, HALF:] = corner[QUARTER:]


def send_kernel(in_ref, send_ref):
    side = lax.axis_index("core")

    @pl.when(side == 0)
    def _():
        right_gram(in_ref, send_ref)

    @pl.when(side == 1)
    def _():
        left_gram(in_ref, send_ref)


def keep_kernel(in_ref, keep_ref, mean_ref):
    side = lax.axis_index("core")

    @pl.when(side == 0)
    def _():
        left_gram(in_ref, keep_ref)

    @pl.when(side == 1)
    def _():
        right_gram(in_ref, keep_ref)

    total = group_block(in_ref, 0).astype(jnp.float32)
    for group in range(1, PER_STRIP):
        total += group_block(in_ref, group).astype(jnp.float32)
    mean_ref[...] = total


def gram(kernel, rows, blocks):
    return pl.pallas_call(
        kernel,
        out_shape=[jax.ShapeDtypeStruct((n, BLOCK), jnp.float32) for n in rows],
        compiler_params=pltpu.CompilerParams(vmem_limit_bytes=32 * 1024 * 1024),
        cost_estimate=pl.CostEstimate(
            flops=4 * 2 * BLOCK**3, bytes_accessed=16 * BLOCK * BLOCK, transcendentals=0
        ),
    )(blocks)


def root_kernel(own_ref, other_ref, out_ref, packed_ref):
    row = lax.broadcasted_iota(jnp.int32, (QUARTER, QUARTER), 0)
    col = lax.broadcasted_iota(jnp.int32, (QUARTER, QUARTER), 1)
    diagonal = row == col
    tiles = [slice(start, start + QUARTER) for start in range(0, BLOCK, QUARTER)]
    packed = own_ref[...] + other_ref[...]
    low = jnp.concatenate([packed[HALF:, :HALF], packed[HALF:, HALF:]], axis=0)
    low = jnp.concatenate([packed[:HALF, HALF:].T, low], axis=1)
    stat = jnp.concatenate([packed[:HALF], low], axis=0)
    on_diagonal = sum(jnp.where(diagonal, stat[tile, tile], 0.0) for tile in tiles)
    trace = jnp.sum(on_diagonal, keepdims=True)
    growth = 1.25**4
    f = stat * (0.2 / trace)
    y = None
    for iteration in range(ITERS - 1):
        fb = f.astype(jnp.bfloat16)
        f_squared = dot_nn(fb, fb)
        g = 2.0 * f - f_squared
        gb = g.astype(jnp.bfloat16)
        h = 2.0 * g - dot_nn(gb, gb)
        hb = h.astype(jnp.bfloat16)
        if iteration + 2 < ITERS:
            y = f if y is None else y + f - dot_nn(y.astype(jnp.bfloat16), fb)
            hf = split_product(h, f) if iteration == 0 else dot_nn(hb, fb)
            f = growth * (f - hf)
        else:
            af = f - f_squared
            w = f + growth * (af - dot_nn(hb, af.astype(jnp.bfloat16)))
            y = y + w - dot_nn(y.astype(jnp.bfloat16), w.astype(jnp.bfloat16))
    scale = lax.rsqrt(jnp.sqrt(trace * (1.0 / (GROUPS * BLOCK)))) * 1.25**ITERS
    out_ref[...] = (-scale * y).astype(jnp.bfloat16)
    for tile in tiles:
        x = scale * (jnp.where(diagonal, 1.0, 0.0) - y[tile, tile])
        out_ref[tile, tile] = x.astype(jnp.bfloat16)
    store_gram(out_ref[:HALF], out_ref[HALF:, HALF:], packed_ref)


def inverse_root(own, other):
    return pl.pallas_call(
        root_kernel,
        out_shape=[
            jax.ShapeDtypeStruct((n, BLOCK), jnp.bfloat16) for n in (BLOCK, HALF + QUARTER)
        ],
        compiler_params=pltpu.CompilerParams(vmem_limit_bytes=48 * 1024 * 1024),
        cost_estimate=pl.CostEstimate(
            flops=20 * 2 * BLOCK**3, bytes_accessed=10 * BLOCK * BLOCK, transcendentals=0
        ),
    )(own, other)


def mean_kernel(own_ref, other_ref, out_ref):
    out_ref[...] = ((own_ref[...] + other_ref[...]) * (1.0 / GROUPS)).astype(jnp.bfloat16)


def mean_block(own, other):
    return pl.pallas_call(
        mean_kernel,
        out_shape=jax.ShapeDtypeStruct((BLOCK, BLOCK), jnp.bfloat16),
        compiler_params=pltpu.CompilerParams(vmem_limit_bytes=16 * 1024 * 1024),
        cost_estimate=pl.CostEstimate(
            flops=2 * BLOCK * BLOCK, bytes_accessed=10 * BLOCK * BLOCK, transcendentals=0
        ),
    )(own, other)


def update_kernel(own_ref, other_ref, mean_ref, out_ref):
    side = lax.axis_index("core")

    packed = other_ref[...]
    low = jnp.concatenate([packed[HALF:, :HALF], packed[HALF:, HALF:]], axis=0)
    low = jnp.concatenate([packed[:HALF, HALF:].T, low], axis=1)
    other = jnp.concatenate([packed[:HALF], low], axis=0)

    def piece(left, right):
        inner = dot_nn(mean_ref[...], right).astype(jnp.bfloat16)
        out_ref[...] = dot_nn(left, inner).astype(jnp.bfloat16)

    @pl.when(side == 0)
    def _():
        piece(own_ref[...], other[:, :HALF])

    @pl.when(side == 1)
    def _():
        piece(other, own_ref[:, HALF:])


def update_piece(own, other, mean):
    return pl.pallas_call(
        update_kernel,
        out_shape=jax.ShapeDtypeStruct((BLOCK, HALF), jnp.bfloat16),
        compiler_params=pltpu.CompilerParams(vmem_limit_bytes=32 * 1024 * 1024),
    )(own, other, mean)


def swap_cores(x):
    return lax.ppermute(x, "core", [(0, 1), (1, 0)])


def per_device(gradients):
    send = relayout(gradients[0])
    arrived = lax.all_to_all(send, ("y", "z", "x"), split_axis=0, concat_axis=0, tiled=True)
    blocks = arrived.reshape(STRIPS, PER_STRIP, 16, BLOCK)
    (other,) = gram(send_kernel, (HALF + QUARTER,), blocks)
    stat_other = swap_cores(other)
    keep, mean_own = gram(keep_kernel, (HALF + QUARTER, BLOCK), blocks)
    mean_other = swap_cores(mean_own)
    own_root, packed_root = inverse_root(keep, stat_other)
    other_root = swap_cores(packed_root)
    piece = update_piece(own_root, other_root, mean_block(mean_own, mean_other))
    rows = lax.all_to_all(
        piece.reshape(STRIPS, 16, HALF), ("y", "z"), split_axis=0, concat_axis=0, tiled=True
    )
    return jnp.swapaxes(rows, 0, 1)[:, :, None, :]


def solution(mesh):
    fine = Mesh(mesh.devices.reshape(4, 2, 4, 8), ("x", "core", "y", "z"))
    return jax.shard_map(
        per_device,
        mesh=fine,
        in_specs=(P(("x", "core"), ("y", "z"), None),),
        out_specs=P(("y", "z"), None, ("x", "core"), None),
        check_vma=False,
    )
```
